32 devices in a mesh: node: 8 (over y, x, core), local: 4 (over z).
Axes of the slice: x: 2, y: 2, z: 4, core: 2. Of those that a mesh axis runs over, the one named last changes fastest.
Arguments:
- grads: bfloat16 [4096, 5376], P(('node', 'local')), may hold values from -6 to 6
- token_slot: int32 [4096], P(('node', 'local')), may hold values from 0 to 63, as said below
- node_ids: int32 [8, 64], P('node', 'local'), may hold values from 0 to 262143, as said below
- touched_ids: int32 [512], P(('node', 'local')), may hold values from -1 to 262143, as said below
- owner_map: int32 [32, 8, 2], P(('node', 'local')), may hold values from -1 to 15, as said below
- moment: float32 [512, 5376], P(('node', 'local')), may hold values from -4 to 4
- second: float32 [512, 5376], P(('node', 'local')), may hold values from 0.01 to 1
- master: float32 [512, 5376], P(('node', 'local')), may hold values from -0.12 to 0.12
Outputs:
- token_rows: bfloat16 [4096, 5376], P(('node', 'local'))
- moment_out: float32 [512, 5376], P(('node', 'local'))
- second_out: float32 [512, 5376], P(('node', 'local'))
- master_out: float32 [512, 5376], P(('node', 'local'))
The draws below stay inside these ranges and needn't reach their ends.
Inputs may be any that keep to these rules, and one draw needn't show every extreme that they name: `node_ids`: within one device's 16 entries the ids are distinct and at most 2 of them share an owner node id // 32768; for each local index one owner node receives exactly 2 ids from every node's device of that local index. `token_slot`: every entry of a node's list is used by some token of that node. `touched_ids`: on device (o, j) the entries that are not -1 are distinct ids with owner node o, and they are exactly the ids that devices of local index j list with owner node o. `owner_map`: on device (o, j), entry [n, c] is the position in this device's touched_ids of the c-th id, in list order, that device (n, j) lists with owner node o, and -1 where device (n, j) lists fewer than c + 1 such ids.
All inputs are finite; a program needn't handle non-finite values.
Results may differ from the reference program's by a relative error of at most 0.014.
Values may be sent and summed in bfloat16 or wider, within the bound.
A program may use at most 64 MiB of HBM per device.

```python
import math
import jax
import jax.numpy as jnp
from jax import lax

D = 5376
VOCAB = 262144
TOK_DEV = 128
SLOT_DEV = 16
CAP = 2
TOUCH_CAP = 16
STEP = 100
TOKENS = 4096
TOUCHED = 512
N_NODE = 8
N_LOCAL = 4


def layout(key):
    subkeys = jax.random.split(key, 8)
    dest_slots = N_NODE * CAP
    rows_node = VOCAB // N_NODE
    reach = rows_node // N_LOCAL
    local_range = jnp.arange(N_LOCAL, dtype=jnp.int32)
    crowded = jnp.where(local_range == N_LOCAL - 1, N_NODE - 1, jax.random.randint(subkeys[0], (N_LOCAL,), 0, N_NODE))
    slot_owner = jnp.arange(dest_slots, dtype=jnp.int32) // CAP
    preference = (slot_owner[None, None, :] == crowded[None, :, None]).astype(jnp.int32) * (1 << 29)
    scores = jax.random.randint(subkeys[1], (N_NODE, N_LOCAL, dest_slots), 0, 1 << 20) * dest_slots + jnp.arange(dest_slots, dtype=jnp.int32)
    chosen = lax.top_k(scores + preference, SLOT_DEV)[1]
    mixing = jax.random.randint(subkeys[2], (N_NODE, N_LOCAL, SLOT_DEV), 0, 1 << 20) * SLOT_DEV + jnp.arange(SLOT_DEV, dtype=jnp.int32)
    shuffled = lax.top_k(mixing, SLOT_DEV)[1]
    target = jnp.take_along_axis(chosen, shuffled, axis=2) // CAP
    same_owner = target[:, :, :, None] == target[:, :, None, :]
    positions = jnp.arange(SLOT_DEV, dtype=jnp.int32)
    earlier = positions[None, :] < positions[:, None]
    rank_slot = jnp.sum((same_owner & earlier[None, None]).astype(jnp.int32), axis=3)
    first_pos = jnp.minimum(jax.random.randint(subkeys[3], (N_NODE, N_LOCAL, N_NODE), 0, TOUCH_CAP), jax.random.randint(subkeys[4], (N_NODE, N_LOCAL, N_NODE), 0, TOUCH_CAP))
    stride = 1 + jax.random.randint(subkeys[5], (N_NODE, N_LOCAL, N_NODE), 0, TOUCH_CAP - 1)
    shift_pos = jax.random.randint(subkeys[6], (N_LOCAL,), 0, TOUCH_CAP)
    spread_pos = (jnp.take_along_axis(first_pos, target, axis=2) + rank_slot * jnp.take_along_axis(stride, target, axis=2)) % TOUCH_CAP
    node_index = jnp.arange(N_NODE, dtype=jnp.int32)[:, None, None]
    local_index = local_range[None, :, None]
    packed_pos = (node_index * CAP + rank_slot + shift_pos[None, :, None]) % TOUCH_CAP
    position = jnp.where(target == crowded[None, :, None], packed_pos, spread_pos)
    owner_device = target * N_LOCAL + local_index
    flat_map = (owner_device * N_NODE + node_index) * CAP + rank_slot
    owner_map = jnp.full((N_NODE * N_LOCAL * N_NODE * CAP,), -1, jnp.int32).at[flat_map.reshape(-1)].set(position.reshape(-1))
    touched_flat = (owner_device * TOUCH_CAP + position).reshape(-1)
    occupied = jnp.zeros((N_NODE * N_LOCAL * TOUCH_CAP,), jnp.int32).at[touched_flat].max(1)
    reach_index = jnp.arange(reach, dtype=jnp.int32)[None, :]
    row_scores = jax.random.randint(subkeys[7], (N_NODE * N_LOCAL, reach), 0, 1 << 14) * reach + reach_index
    row_scores = row_scores + (reach_index == reach - 1).astype(jnp.int32) * (1 << 30)
    picks = lax.top_k(row_scores, TOUCH_CAP)[1]
    touch_index = jnp.arange(TOUCH_CAP, dtype=jnp.int32)[None, :]
    occupied_rows = occupied.reshape(N_NODE * N_LOCAL, TOUCH_CAP)
    first_occ = jnp.min(jnp.where(occupied_rows > 0, touch_index, TOUCH_CAP), axis=1) % TOUCH_CAP
    pick_order = (touch_index - first_occ[:, None]) % TOUCH_CAP
    placed_picks = jnp.take_along_axis(picks, pick_order, axis=1)
    device_index = jnp.arange(N_NODE * N_LOCAL, dtype=jnp.int32)
    owner_ids = (device_index // N_LOCAL)[:, None] * rows_node + (device_index % N_LOCAL)[:, None] + N_LOCAL * placed_picks
    owner_ids = owner_ids.reshape(-1).astype(jnp.int32)
    touched = jnp.where(occupied > 0, owner_ids, -1).astype(jnp.int32)
    node_ids = owner_ids[touched_flat].reshape(N_NODE, N_LOCAL * SLOT_DEV)
    return (node_ids, touched, owner_map.reshape(N_NODE * N_LOCAL, N_NODE, CAP))


def draw_node_ids(key, part):
    listed, touched, mapping = layout(key)
    return listed


def draw_touched_ids(key, part):
    listed, touched, mapping = layout(key)
    return touched


def draw_owner_map(key, part):
    listed, touched, mapping = layout(key)
    return mapping


def draw_token_slot(key, part):
    key = jax.random.fold_in(key, 11)
    list_len = N_LOCAL * SLOT_DEV
    node_tokens = N_LOCAL * TOK_DEV
    key_one, key_two, key_three, key_four = jax.random.split(key, 4)
    shape = (N_NODE, node_tokens)
    drawn_slot = jnp.minimum(jax.random.randint(key_one, shape, 0, list_len), jax.random.randint(key_two, shape, 0, list_len))
    token_index = jnp.arange(node_tokens, dtype=jnp.int32)[None, :]
    drawn_slot = jnp.where(token_index < list_len, token_index % list_len, drawn_slot)
    slot_scores = jax.random.randint(key_three, (N_NODE, list_len), 0, 1 << 16) * list_len + jnp.arange(list_len, dtype=jnp.int32)[None, :]
    slot_order = lax.top_k(slot_scores, list_len)[1]
    mapped = jnp.take_along_axis(slot_order, drawn_slot, axis=1)
    token_scores = jax.random.randint(key_four, shape, 0, 1 << 16) * node_tokens + token_index
    token_order = lax.top_k(token_scores, node_tokens)[1]
    placed = jnp.take_along_axis(mapped, token_order, axis=1)
    return placed.reshape(-1).astype(jnp.int32)


def block_levels(stream_key, shape, pieces, least, top_value):
    gain = 1.0
    for dim, parts in pieces:
        draws = jax.random.uniform(jax.random.fold_in(jax.random.fold_in(stream_key, 6), dim), (parts,), jnp.float32, least / len(pieces), top_value / len(pieces))
        gain = gain * jnp.repeat(jnp.exp(draws), shape[dim] // parts).reshape((-1,) + (1,) * (len(shape) - 1 - dim))
    return gain


def centred(key, extent, deviation, most, pieces=(), kind=jnp.bfloat16):
    result = jax.random.normal(key, extent, jnp.float32) * deviation
    if len(pieces) > 0:
        result = block_levels(key, extent, pieces, -0.22, 0.18) * result
    return jnp.clip(result, min=-most, max=most).astype(kind)


def setup_inputs(seed: int = 0) -> dict:
    arg_keys = jax.random.split(jax.random.key(seed), 9)
    grads = centred(arg_keys[0], (TOKENS, D), 1.0, 6.0, ((0, 32),))
    token_slot = draw_token_slot(jax.random.fold_in(arg_keys[8], 71), 0)
    node_ids = draw_node_ids(jax.random.fold_in(arg_keys[8], 71), 0)
    touched_ids = draw_touched_ids(jax.random.fold_in(arg_keys[8], 71), 0)
    owner_map = draw_owner_map(jax.random.fold_in(arg_keys[8], 71), 0)
    moment = centred(arg_keys[5], (TOUCHED, D), 0.3, 4.0, ((0, 32),), jnp.float32)
    second = jnp.clip(jnp.exp(math.log(1.0) - 4.6051702 * jax.random.uniform(arg_keys[6], (TOUCHED, D), jnp.float32) ** block_levels(arg_keys[6], (TOUCHED, D), ((0, 32),), -0.2, 0.2)), 0.01, 1.0)
    master = centred(arg_keys[7], (TOUCHED, D), 0.02, 0.12, ((0, 32),), jnp.float32)
    return dict(grads=grads, token_slot=token_slot, node_ids=node_ids, touched_ids=touched_ids, owner_map=owner_map, moment=moment, second=second, master=master)


BETA_ONE = 0.9
BETA_TWO = 0.999
LEARN_RATE = 0.01
EPSILON = 1e-08

def adam_rows(gradient, moment, second, master, alive_rows):
    corr_one = 1.0 - BETA_ONE ** STEP
    corr_two = 1.0 - BETA_TWO ** STEP
    moment_new = BETA_ONE * moment + (1.0 - BETA_ONE) * gradient
    second_new = BETA_TWO * second + (1.0 - BETA_TWO) * gradient * gradient
    master_new = master - LEARN_RATE * (moment_new / corr_one) / (jnp.sqrt(second_new / corr_two) + EPSILON)
    kept = alive_rows[:, None]
    return (jnp.where(kept, moment_new, moment), jnp.where(kept, second_new, second), jnp.where(kept, master_new, master))

def reference(grads, token_slot, node_ids, touched_ids, owner_map, moment, second, master):
    list_len = N_LOCAL * SLOT_DEV
    grads_nodes = grads.reshape(N_NODE, N_LOCAL, TOK_DEV, D)
    slots_nodes = token_slot.reshape(N_NODE, N_LOCAL, TOK_DEV)

    def node_block(inputs):
        node_grads, node_slots = inputs

        def one_device(device_grads, device_slots):
            partial_sum = jax.ops.segment_sum(device_grads.astype(jnp.float32), device_slots, num_segments=list_len)
            return partial_sum.astype(jnp.bfloat16)
        partials = jax.vmap(one_device)(node_grads, node_slots)
        return lax.optimization_barrier(jnp.sum(partials.astype(jnp.float32), axis=0)).astype(jnp.bfloat16)
    node_sum = lax.map(node_block, (grads_nodes, slots_nodes))
    listed = node_ids.reshape(N_NODE, N_LOCAL, SLOT_DEV)
    owner_node = (listed // (VOCAB // N_NODE)).astype(jnp.int32)
    same_owner = owner_node[:, :, :, None] == owner_node[:, :, None, :]
    positions = jnp.arange(SLOT_DEV, dtype=jnp.int32)
    earlier = positions[None, :] < positions[:, None]
    rank_slot = lax.optimization_barrier(jnp.sum((same_owner & earlier[None, None]).astype(jnp.int32), axis=3))
    local_index = jnp.arange(N_LOCAL, dtype=jnp.int32)[None, :, None]
    node_index = jnp.arange(N_NODE, dtype=jnp.int32)[:, None, None]
    owner_device = owner_node * N_LOCAL + local_index
    touch_pos = owner_map[owner_device, node_index, rank_slot].astype(jnp.int32)
    target_row = (owner_device * TOUCH_CAP + touch_pos).reshape(-1).astype(jnp.int32)
    gradient = jax.ops.segment_sum(node_sum.reshape(-1, D).astype(jnp.float32), target_row, num_segments=N_NODE * N_LOCAL * TOUCH_CAP)
    moment_out, second_out, master_out = adam_rows(gradient, moment, second, master, touched_ids >= 0)
    fresh_rows = master_out.astype(jnp.bfloat16)
    slot_rows = fresh_rows[target_row]
    token_target = (jnp.arange(N_NODE, dtype=jnp.int32)[:, None] * list_len + slots_nodes.reshape(N_NODE, N_LOCAL * TOK_DEV)).reshape(-1).astype(jnp.int32)
    token_rows = slot_rows[token_target]
    return (token_rows, moment_out, second_out, master_out)
```

```python
import functools

import jax
import jax.numpy as jnp
from jax import lax
from jax.experimental import pallas as pl
from jax.experimental.pallas import tpu as pltpu
from jax.sharding import PartitionSpec as P

VOCAB = 262144
STEP = 100

BETA_ONE = 0.9
BETA_TWO = 0.999
LEARN_RATE = 0.01
EPSILON = 1e-08

MESH = pl.DeviceIdType.MESH
CHUNKS = 3
AHEAD = 2
BLOCKS = 7
TILE = 16
F32 = jnp.float32
BF16 = jnp.bfloat16


def adam_rows(gradient, moment, second, master, kept):
    corr_one = 1.0 - BETA_ONE**STEP
    corr_two = 1.0 - BETA_TWO**STEP
    moment_new = BETA_ONE * moment + (1.0 - BETA_ONE) * gradient
    second_new = BETA_TWO * second + (1.0 - BETA_TWO) * gradient * gradient
    master_new = master - LEARN_RATE * (moment_new / corr_one) / (
        jnp.sqrt(second_new / corr_two) + EPSILON
    )
    return (
        jnp.where(kept, moment_new, moment),
        jnp.where(kept, second_new, second),
        jnp.where(kept, master_new, master),
    )


def repeat(count, body):
    if count <= 8:
        for step in range(count):
            body(step)
    else:
        lax.fori_loop(0, count, lambda step, carry: (body(step), carry)[1], None)


def dot(a, b):
    return jnp.dot(a, b, preferred_element_type=F32)


def kernel(
    nodes,
    locals_,
    cap,
    slot_ref,
    ids_ref,
    touched_ref,
    omap_ref,
    grads_hbm,
    moment_hbm,
    second_hbm,
    master_hbm,
    tok_out,
    moment_out,
    second_out,
    master_out,
    grads,
    moment,
    second,
    master,
    route,
    route_t,
    collect,
    collect_t,
    select,
    select_t,
    part,
    up_src,
    up_dst,
    dn_src,
    dn_dst,
    fwd_src,
    fwd_dst,
    rep_src,
    rep_dst,
    gath,
    load_sem,
    adam_sem,
    up_ss,
    up_rs,
    dn_ss,
    dn_rs,
    fwd_ss,
    fwd_rs,
    rep_ss,
    rep_rs,
    ag_up_ss,
    ag_dn_ss,
    ag_rs,
):
    n = lax.axis_index("node")
    j = lax.axis_index("local")
    last = locals_ - 1
    width = grads.shape[1]
    cw = width // CHUNKS
    bw = cw // BLOCKS
    slots = part.shape[2]
    group = TILE // cap
    stacked = BLOCKS * slots

    loads = []
    for k in range(CHUNKS):
        cols = pl.ds(k * cw, cw)
        loads.append(
            pltpu.make_async_copy(grads_hbm.at[:, cols], grads.at[:, cols], load_sem.at[k])
        )
        loads[-1].start()
    adam_loads = [
        pltpu.make_async_copy(src, dst, adam_sem.at[i])
        for i, (src, dst) in enumerate(
            ((moment_hbm, moment), (second_hbm, second), (master_hbm, master))
        )
    ]
    for copy in adam_loads:
        copy.start()

    barrier = pltpu.get_barrier_semaphore()

    def greet(p):
        pl.semaphore_signal(
            barrier, inc=1, device_id=(lax.rem(n + p + 1, nodes), j), device_id_type=MESH
        )

    @pl.when(j > 0)
    def _():
        pl.semaphore_signal(barrier, inc=1, device_id=(n, j - 1), device_id_type=MESH)

    @pl.when(j < last)
    def _():
        pl.semaphore_signal(barrier, inc=1, device_id=(n, j + 1), device_id_type=MESH)

    repeat(nodes - 1, greet)

    def iota(shape, dim):
        return lax.broadcasted_iota(jnp.int32, shape, dim)

    shape = select.shape
    chosen = jnp.where(iota(shape, 0) == slot_ref[...], 1.0, 0.0).astype(F32)
    select[...] = chosen.astype(BF16)

    ids = ids_ref[...]
    rows_node = VOCAB // nodes
    owner = lax.shift_right_logical(ids, rows_node.bit_length() - 1).astype(F32)
    shape = (slots, stacked)
    sub, lane = iota(shape, 0), iota(shape, 1)
    owner_col = jnp.sum(jnp.where(lane == sub, owner, 0.0), axis=1, keepdims=True)
    earlier = (owner_col == owner) & (sub < lane % slots)
    rank = jnp.sum(jnp.where(earlier, 1.0, 0.0), axis=0, keepdims=True)
    sent = owner * float(cap) + rank
    shape = route.shape
    sub, lane = iota(shape, 0), iota(shape, 1)
    wanted = ((sub // TILE) * cap + (sub % TILE) // group).astype(F32)
    routed = jnp.where((wanted == sent) & (sub % group == lane // slots), 1.0, 0.0).astype(F32)
    route[...] = routed.astype(BF16)

    shape = collect.shape
    sub, lane = iota(shape, 0), iota(shape, 1)
    taken = jnp.where(
        (sub % TILE == omap_ref[...]) & (sub // TILE == lane % group), 1.0, 0.0
    ).astype(F32)
    collect[...] = taken.astype(BF16)

    touch = touched_ref[...].astype(F32)
    shape = (touch.shape[1], touch.shape[1])
    diagonal = iota(shape, 0) == iota(shape, 1)
    kept = jnp.sum(jnp.where(diagonal, touch, 0.0), axis=1, keepdims=True) >= 0.0

    line_peers = jnp.minimum(j, 1) + jnp.minimum(last - j, 1)
    pl.semaphore_wait(barrier, nodes - 1 + line_peers)

    def up_copy(k, s):
        return pltpu.make_async_remote_copy(
            up_src.at[k, s],
            up_dst.at[k, s],
            up_ss.at[k, s],
            up_rs.at[k, s],
            device_id=(n, jnp.minimum(j + 1, last)),
            device_id_type=MESH,
        )

    def dn_copy(k, s):
        return pltpu.make_async_remote_copy(
            dn_src.at[k, s],
            dn_dst.at[k, s],
            dn_ss.at[k, s],
            dn_rs.at[k, s],
            device_id=(n, jnp.maximum(j - 1, 0)),
            device_id_type=MESH,
        )

    def ag_copy(k, t, up):
        return pltpu.make_async_remote_copy(
            gath.at[k, t],
            gath.at[k, t],
            (ag_up_ss if up else ag_dn_ss).at[k, t],
            ag_rs.at[k, t],
            device_id=(n, jnp.minimum(j + 1, last) if up else jnp.maximum(j - 1, 0)),
            device_id_type=MESH,
        )

    def send_nodes(k, src, dst, ss, rs):
        def send(p):
            peer = lax.rem(n + p + 1, nodes)
            pltpu.make_async_remote_copy(
                src.at[k, peer],
                dst.at[k, n],
                ss.at[k],
                rs.at[k],
                device_id=(peer, j),
                device_id_type=MESH,
            ).start()

        repeat(nodes - 1, send)
        dst[k, n] = src[k, n]

    def wait_nodes(k, buf, sem):
        whole = buf.at[k, pl.ds(0, nodes - 1)]
        pltpu.make_async_copy(whole, whole, sem.at[k]).wait()

    def begin(k):
        loads[k].wait()
        sums = dot(select[...], grads[:, k * cw : (k + 1) * cw])
        part[k] = sums.reshape(locals_, slots, cw)

        @pl.when(j == 0)
        def _():
            def step(s):
                up_src[k, s] = part[k, last - s].astype(BF16)
                up_copy(k, s).start()

            repeat(last, step)

        @pl.when(j == last)
        def _():
            def step(s):
                dn_src[k, s] = part[k, s].astype(BF16)
                dn_copy(k, s).start()

            repeat(last, step)

    def relay(k):
        def step(s):
            t = last - s

            @pl.when((j > 0) & (t > j))
            def _():
                up_copy(k, s).wait_recv()
                up_src[k, s] = (up_dst[k, s].astype(F32) + part[k, t]).astype(BF16)
                up_copy(k, s).start()

            @pl.when((j < last) & (s < j))
            def _():
                dn_copy(k, s).wait_recv()
                dn_src[k, s] = (dn_dst[k, s].astype(F32) + part[k, s]).astype(BF16)
                dn_copy(k, s).start()

        repeat(last, step)

        @pl.when(j > 0)
        def _():
            up_copy(k, last - j).wait_recv()
            part[k, j] = part[k, j] + up_dst[k, last - j].astype(F32)

        @pl.when(j < last)
        def _():
            dn_copy(k, j).wait_recv()
            part[k, j] = part[k, j] + dn_dst[k, j].astype(F32)

        own = part[k, j].astype(BF16)
        tall = jnp.concatenate([own[:, b * bw : (b + 1) * bw] for b in range(BLOCKS)], axis=0)
        fwd_src[k] = dot(route[...], tall).astype(BF16).reshape(nodes, TILE, bw)
        send_nodes(k, fwd_src, fwd_dst, fwd_ss, fwd_rs)

    def update(k):
        if k == 0:
            for copy in adam_loads:
                copy.wait()
        wait_nodes(k, fwd_dst, fwd_rs)
        gradient = dot(collect[...], fwd_dst[k].reshape(nodes * TILE, bw))
        fresh = []
        for b in range(BLOCKS):
            cols = slice(k * cw + b * bw, k * cw + (b + 1) * bw)
            new = adam_rows(
                gradient[b * TILE : (b + 1) * TILE],
                moment[:, cols],
                second[:, cols],
                master[:, cols],
                kept,
            )
            moment_out[:, cols], second_out[:, cols], master_out[:, cols] = new
            fresh.append(new[2].astype(BF16))
        tall = jnp.concatenate(fresh, axis=0)
        rep_src[k] = dot(collect_t[...], tall).astype(BF16).reshape(nodes, TILE, bw)
        send_nodes(k, rep_src, rep_dst, rep_ss, rep_rs)

    def listed(k):
        wait_nodes(k, rep_dst, rep_rs)
        rows = dot(route_t[...], rep_dst[k].reshape(nodes * TILE, bw)).astype(BF16)
        for b in range(BLOCKS):
            gath[k, j, :, b * bw : (b + 1) * bw] = rows[b * slots : (b + 1) * slots]

        @pl.when(j < last)
        def _():
            ag_copy(k, j, True).start()

        @pl.when(j > 0)
        def _():
            ag_copy(k, j, False).start()

    def spread(k):
        def step(d):
            low, high = j - 1 - d, j + 1 + d

            @pl.when(low >= 0)
            def _():
                ag_copy(k, low, True).wait_recv()

                @pl.when(j < last)
                def _():
                    ag_copy(k, low, True).start()

            @pl.when(high <= last)
            def _():
                ag_copy(k, high, False).wait_recv()

                @pl.when(j > 0)
                def _():
                    ag_copy(k, high, False).start()

        repeat(last, step)
        rows = gath[k].reshape(locals_ * slots, cw)
        tok_out[:, k * cw : (k + 1) * cw] = dot(select_t[...], rows).astype(BF16)

    for k in range(min(AHEAD, CHUNKS)):
        begin(k)
    route_t[...] = routed.T.astype(BF16)
    collect_t[...] = taken.T.astype(BF16)
    select_t[...] = chosen.T.astype(BF16)
    for tick in range(CHUNKS + 3):
        if tick < CHUNKS:
            relay(tick)
        if tick + AHEAD < CHUNKS:
            begin(tick + AHEAD)
        if 0 <= tick - 1 < CHUNKS:
            update(tick - 1)
        if 0 <= tick - 2 < CHUNKS:
            listed(tick - 2)
        if 0 <= tick - 3 < CHUNKS:
            spread(tick - 3)

    for k in range(CHUNKS):
        wait_nodes(k, fwd_src, fwd_ss)
        wait_nodes(k, rep_src, rep_ss)

        def drain(s):
            @pl.when(last - s > j)
            def _():
                up_copy(k, s).wait_send()

            @pl.when(s < j)
            def _():
                dn_copy(k, s).wait_send()

        repeat(last, drain)

        def drain_gather(t):
            @pl.when((t <= j) & (j < last))
            def _():
                ag_copy(k, t, True).wait_send()

            @pl.when((t >= j) & (j > 0))
            def _():
                ag_copy(k, t, False).wait_send()

        repeat(locals_, drain_gather)


def on_device(nodes, locals_, grads, token_slot, node_ids, touched_ids, owner_map, moment, second, master):
    tokens, width = grads.shape
    slots = node_ids.shape[1]
    touch = touched_ids.shape[0]
    cap = owner_map.shape[2]
    group = TILE // cap
    cw = width // CHUNKS
    bw = cw // BLOCKS
    last = locals_ - 1
    vmem = pl.BlockSpec(memory_space=pltpu.VMEM)
    hbm = pl.BlockSpec(memory_space=pl.ANY)
    dma = pltpu.SemaphoreType.DMA
    outs = (
        jax.ShapeDtypeStruct((tokens, width), BF16),
        jax.ShapeDtypeStruct((touch, width), F32),
        jax.ShapeDtypeStruct((touch, width), F32),
        jax.ShapeDtypeStruct((touch, width), F32),
    )
    line = pltpu.VMEM((CHUNKS, last, slots, cw), BF16)
    plane = pltpu.VMEM((CHUNKS, nodes, TILE, bw), BF16)
    stacked = BLOCKS * slots
    return pl.pallas_call(
        functools.partial(kernel, nodes, locals_, cap),
        out_shape=outs,
        in_specs=[vmem] * 4 + [hbm] * 4,
        out_specs=[vmem] * 4,
        scratch_shapes=[
            pltpu.VMEM((tokens, width), BF16),
            pltpu.VMEM((touch, width), F32),
            pltpu.VMEM((touch, width), F32),
            pltpu.VMEM((touch, width), F32),
            pltpu.VMEM((nodes * TILE, stacked), BF16),
            pltpu.VMEM((stacked, nodes * TILE), BF16),
            pltpu.VMEM((BLOCKS * touch, nodes * TILE), BF16),
            pltpu.VMEM((nodes * TILE, BLOCKS * touch), BF16),
            pltpu.VMEM((locals_ * slots, tokens), BF16),
            pltpu.VMEM((tokens, locals_ * slots), BF16),
            pltpu.VMEM((CHUNKS, locals_, slots, cw), F32),
            line,
            line,
            line,
            line,
            plane,
            plane,
            plane,
            plane,
            pltpu.VMEM((CHUNKS, locals_, slots, cw), BF16),
            dma((CHUNKS,)),
            dma((3,)),
            dma((CHUNKS, last)),
            dma((CHUNKS, last)),
            dma((CHUNKS, last)),
            dma((CHUNKS, last)),
            dma((CHUNKS,)),
            dma((CHUNKS,)),
            dma((CHUNKS,)),
            dma((CHUNKS,)),
            dma((CHUNKS, locals_)),
            dma((CHUNKS, locals_)),
            dma((CHUNKS, locals_)),
        ],
        compiler_params=pltpu.CompilerParams(
            collective_id=0, has_side_effects=True, vmem_limit_bytes=56 * 1024 * 1024
        ),
    )(
        token_slot.reshape(1, tokens),
        jnp.tile(node_ids, (1, BLOCKS)),
        touched_ids.reshape(1, touch),
        jnp.repeat(owner_map.reshape(1, nodes * cap), group, axis=1),
        grads,
        moment,
        second,
        master,
    )


def solution(mesh):
    nodes, locals_ = mesh.shape["node"], mesh.shape["local"]
    placed = (
        P(("node", "local"), None),
        P(("node", "local")),
        P("node", "local"),
        P(("node", "local")),
        P(("node", "local"), None, None),
        P(("node", "local"), None),
        P(("node", "local"), None),
        P(("node", "local"), None),
    )
    return jax.shard_map(
        functools.partial(on_device, nodes, locals_),
        mesh=mesh,
        in_specs=placed,
        out_specs=(P(("node", "local"), None),) * 4,
        check_vma=False,
    )
```

```python
import functools

import jax
import jax.numpy as jnp
from jax import lax
from jax.experimental import pallas as pl
from jax.experimental.pallas import tpu as pltpu
from jax.sharding import PartitionSpec as P

VOCAB = 262144
STEP = 100

BETA_ONE = 0.9
BETA_TWO = 0.999
LEARN_RATE = 0.01
EPSILON = 1e-08

MESH = pl.DeviceIdType.MESH
CHUNKS = 3
BLOCKS = 7
TILE = 16
F32 = jnp.float32
BF16 = jnp.bfloat16


def adam_rows(gradient, moment, second, master, kept):
    corr_one = 1.0 - BETA_ONE**STEP
    corr_two = 1.0 - BETA_TWO**STEP
    moment_new = BETA_ONE * moment + (1.0 - BETA_ONE) * gradient
    second_new = BETA_TWO * second + (1.0 - BETA_TWO) * gradient * gradient
    master_new = master - LEARN_RATE * (moment_new / corr_one) / (
        jnp.sqrt(second_new / corr_two) + EPSILON
    )
    return (
        jnp.where(kept, moment_new, moment),
        jnp.where(kept, second_new, second),
        jnp.where(kept, master_new, master),
    )


def repeat(count, body):
    if count <= 8:
        for step in range(count):
            body(step)
    else:
        lax.fori_loop(0, count, lambda step, carry: (body(step), carry)[1], None)


def dot(a, b):
    return jnp.dot(a, b, preferred_element_type=F32)


def kernel(
    nodes,
    locals_,
    cap,
    slot_ref,
    ids_ref,
    touched_ref,
    omap_ref,
    grads_hbm,
    moment_hbm,
    second_hbm,
    master_hbm,
    gath,
    gradient_out,
    grads,
    moment,
    second,
    master,
    route,
    route_t,
    collect,
    collect_t,
    select,
    part,
    up_src,
    up_dst,
    dn_src,
    dn_dst,
    fwd_src,
    fwd_dst,
    rep_src,
    rep_dst,
    load_sem,
    adam_sem,
    up_ss,
    up_rs,
    dn_ss,
    dn_rs,
    fwd_ss,
    fwd_rs,
    rep_ss,
    rep_rs,
    ag_up_ss,
    ag_dn_ss,
    ag_rs,
):
    n = lax.axis_index("node")
    j = lax.axis_index("local")
    last = locals_ - 1
    half = locals_ // 2
    width = grads.shape[1]
    cw = width // CHUNKS
    bw = cw // BLOCKS
    slots = part.shape[2]
    group = TILE // cap
    stacked = BLOCKS * slots

    loads = []
    for k in range(CHUNKS):
        cols = pl.ds(k * cw, cw)
        loads.append(
            pltpu.make_async_copy(grads_hbm.at[:, cols], grads.at[:, cols], load_sem.at[k])
        )
        loads[-1].start()
    adam_loads = [
        pltpu.make_async_copy(src, dst, adam_sem.at[i])
        for i, (src, dst) in enumerate(
            ((moment_hbm, moment), (second_hbm, second), (master_hbm, master))
        )
    ]
    for copy in adam_loads:
        copy.start()

    barrier = pltpu.get_barrier_semaphore()

    def greet(p):
        pl.semaphore_signal(
            barrier, inc=1, device_id=(lax.rem(n + p + 1, nodes), j), device_id_type=MESH
        )

    @pl.when(j > 0)
    def _():
        pl.semaphore_signal(barrier, inc=1, device_id=(n, j - 1), device_id_type=MESH)

    @pl.when(j < last)
    def _():
        pl.semaphore_signal(barrier, inc=1, device_id=(n, j + 1), device_id_type=MESH)

    repeat(nodes - 1, greet)

    def iota(shape, dim):
        return lax.broadcasted_iota(jnp.int32, shape, dim)

    def column(row, size):
        diagonal = iota((size, size), 0) == iota((size, size), 1)
        return jnp.sum(jnp.where(diagonal, row, 0.0), axis=1, keepdims=True)

    shape = select.shape
    select[...] = jnp.where(iota(shape, 0) == slot_ref[...], 1.0, 0.0).astype(BF16)

    rows_node = VOCAB // nodes
    owner = lax.shift_right_logical(ids_ref[...], rows_node.bit_length() - 1).astype(F32)
    shape = (slots, slots)
    earlier = (column(owner, slots) == owner) & (iota(shape, 0) < iota(shape, 1))
    rank = jnp.sum(jnp.where(earlier, 1.0, 0.0), axis=0, keepdims=True)
    sent = column(owner * float(cap) + rank, slots)
    shape = (slots, stacked)
    sent = jnp.sum(
        jnp.where(iota(shape, 0) == iota(shape, 1) % slots, sent, 0.0), axis=0, keepdims=True
    )
    shape = route.shape
    sub, lane = iota(shape, 0), iota(shape, 1)
    wanted = ((sub // TILE) * cap + (sub % TILE) // group).astype(F32)
    routed = jnp.where((wanted == sent) & (sub % group == lane // slots), 1.0, 0.0).astype(F32)
    route[...] = routed.astype(BF16)

    shape = (nodes, nodes * TILE)
    sub, lane = iota(shape, 0), iota(shape, 1)
    place = jnp.zeros((1, nodes * TILE), F32)
    for c in range(cap):
        held = column(omap_ref[c : c + 1, :].astype(F32), nodes)
        here = (sub == lane // TILE) & ((lane % TILE) // group == c)
        place = place + jnp.sum(jnp.where(here, held, 0.0), axis=0, keepdims=True)
    shape = collect.shape
    sub, lane = iota(shape, 0), iota(shape, 1)
    taken = jnp.where(
        ((sub % TILE).astype(F32) == place) & (sub // TILE == lane % group), 1.0, 0.0
    ).astype(F32)
    collect[...] = taken.astype(BF16)

    kept = column(touched_ref[...].astype(F32), touched_ref.shape[1]) >= 0.0

    line_peers = jnp.minimum(j, 1) + jnp.minimum(last - j, 1)
    pl.semaphore_wait(barrier, nodes - 1 + line_peers)

    def up_copy(k, s):
        return pltpu.make_async_remote_copy(
            up_src.at[k, s],
            up_dst.at[k, s],
            up_ss.at[k, s],
            up_rs.at[k, s],
            device_id=(n, jnp.minimum(j + 1, last)),
            device_id_type=MESH,
        )

    def dn_copy(k, s):
        return pltpu.make_async_remote_copy(
            dn_src.at[k, s],
            dn_dst.at[k, s],
            dn_ss.at[k, s],
            dn_rs.at[k, s],
            device_id=(n, jnp.maximum(j - 1, 0)),
            device_id_type=MESH,
        )

    def ag_copy(k, t, up):
        rows = gath.at[pl.ds(pl.multiple_of(t * slots, slots), slots), pl.ds(k * cw, cw)]
        return pltpu.make_async_remote_copy(
            rows,
            rows,
            (ag_up_ss if up else ag_dn_ss).at[k, t],
            ag_rs.at[k, t],
            device_id=(n, jnp.minimum(j + 1, last) if up else jnp.maximum(j - 1, 0)),
            device_id_type=MESH,
        )

    def send_nodes(k, src, dst, ss, rs):
        def send(p):
            peer = lax.rem(n + p + 1, nodes)
            pltpu.make_async_remote_copy(
                src.at[k, peer],
                dst.at[k, n],
                ss.at[k],
                rs.at[k],
                device_id=(peer, j),
                device_id_type=MESH,
            ).start()

        repeat(nodes - 1, send)
        dst[k, n] = src[k, n]

    def wait_nodes(k, buf, sem):
        whole = buf.at[k, pl.ds(0, nodes - 1)]
        pltpu.make_async_copy(whole, whole, sem.at[k]).wait()

    def begin(k):
        loads[k].wait()
        sums = dot(select[...], grads[:, k * cw : (k + 1) * cw])
        part[k] = sums.reshape(locals_, slots, cw)

        @pl.when(j == 0)
        def _():
            def step(s):
                up_src[k, s] = part[k, last - s].astype(BF16)
                up_copy(k, s).start()

            repeat(last, step)

        @pl.when(j == last)
        def _():
            def step(s):
                dn_src[k, s] = part[k, s].astype(BF16)
                dn_copy(k, s).start()

            repeat(last, step)

    def up_relay(k):
        def step(s):
            @pl.when(last - s > j)
            def _():
                up_copy(k, s).wait_recv()
                up_src[k, s] = (up_dst[k, s].astype(F32) + part[k, last - s]).astype(BF16)
                up_copy(k, s).start()

        repeat(last, step)

    def dn_relay(k):
        def step(s):
            @pl.when(s < j)
            def _():
                dn_copy(k, s).wait_recv()
                dn_src[k, s] = (dn_dst[k, s].astype(F32) + part[k, s]).astype(BF16)
                dn_copy(k, s).start()

        repeat(last, step)

    def near(k):
        pl.when((j > 0) & (j < half))(lambda: up_relay(k))
        pl.when((j < last) & (j >= half))(lambda: dn_relay(k))

    def far(k):
        pl.when((j > 0) & (j < half))(lambda: dn_relay(k))
        pl.when((j < last) & (j >= half))(lambda: up_relay(k))

    def forward(k):
        @pl.when(j > 0)
        def _():
            up_copy(k, last - j).wait_recv()
            part[k, j] = part[k, j] + up_dst[k, last - j].astype(F32)

        @pl.when(j < last)
        def _():
            dn_copy(k, j).wait_recv()
            part[k, j] = part[k, j] + dn_dst[k, j].astype(F32)

        own = part[k, j].astype(BF16)
        tall = jnp.concatenate([own[:, b * bw : (b + 1) * bw] for b in range(BLOCKS)], axis=0)
        fwd_src[k] = dot(route[...], tall).astype(BF16).reshape(nodes, TILE, bw)
        send_nodes(k, fwd_src, fwd_dst, fwd_ss, fwd_rs)

    def update(k):
        if k == 0:
            for copy in adam_loads:
                copy.wait()
        wait_nodes(k, fwd_dst, fwd_rs)
        gradient = dot(collect[...], fwd_dst[k].reshape(nodes * TILE, bw))
        fresh = []
        for b in range(BLOCKS):
            cols = slice(k * cw + b * bw, k * cw + (b + 1) * bw)
            new = adam_rows(
                gradient[b * TILE : (b + 1) * TILE],
                moment[:, cols],
                second[:, cols],
                master[:, cols],
                kept,
            )
            gradient_out[:, cols] = gradient[b * TILE : (b + 1) * TILE]
            fresh.append(new[2].astype(BF16))
        tall = jnp.concatenate(fresh, axis=0)
        rep_src[k] = dot(collect_t[...], tall).astype(BF16).reshape(nodes, TILE, bw)
        send_nodes(k, rep_src, rep_dst, rep_ss, rep_rs)

    def listed(k):
        wait_nodes(k, rep_dst, rep_rs)
        rows = dot(route_t[...], rep_dst[k].reshape(nodes * TILE, bw)).astype(BF16)
        own = pl.ds(pl.multiple_of(j * slots, slots), slots)
        for b in range(BLOCKS):
            cols = slice(k * cw + b * bw, k * cw + (b + 1) * bw)
            gath[own, cols] = rows[b * slots : (b + 1) * slots]

        @pl.when(j < last)
        def _():
            ag_copy(k, j, True).start()

        @pl.when(j > 0)
        def _():
            ag_copy(k, j, False).start()

    def pass_on(k, d):
        low, high = j - 1 - d, j + 1 + d

        @pl.when(low >= 0)
        def _():
            ag_copy(k, low, True).wait_recv()

            @pl.when(j < last)
            def _():
                ag_copy(k, low, True).start()

        @pl.when(high <= last)
        def _():
            ag_copy(k, high, False).wait_recv()

            @pl.when(j > 0)
            def _():
                ag_copy(k, high, False).start()

    def first_hop(k):
        pass_on(k, 0)

    def middle_hops(k):
        repeat(last - 2, lambda d: pass_on(k, d + 1))

    def last_hop(k):
        pass_on(k, last - 1)

    for k in range(CHUNKS):
        begin(k)
    route_t[...] = routed.T.astype(BF16)
    collect_t[...] = taken.T.astype(BF16)
    stages = (near, far, forward, update, listed, first_hop, middle_hops, last_hop)
    for tick in range(CHUNKS + len(stages) - 1):
        for depth in reversed(range(len(stages))):
            if 0 <= tick - depth < CHUNKS:
                stages[depth](tick - depth)

    for k in range(CHUNKS):
        wait_nodes(k, fwd_src, fwd_ss)
        wait_nodes(k, rep_src, rep_ss)

        def drain(s):
            @pl.when(last - s > j)
            def _():
                up_copy(k, s).wait_send()

            @pl.when(s < j)
            def _():
                dn_copy(k, s).wait_send()

        repeat(last, drain)

        def drain_gather(t):
            @pl.when((t <= j) & (j < last))
            def _():
                ag_copy(k, t, True).wait_send()

            @pl.when((t >= j) & (j > 0))
            def _():
                ag_copy(k, t, False).wait_send()

        repeat(locals_, drain_gather)


def on_device(nodes, locals_, grads, token_slot, node_ids, touched_ids, owner_map, moment, second, master):
    tokens, width = grads.shape
    slots = node_ids.shape[1]
    touch = touched_ids.shape[0]
    cap = owner_map.shape[2]
    group = TILE // cap
    cw = width // CHUNKS
    bw = cw // BLOCKS
    last = locals_ - 1
    vmem = pl.BlockSpec(memory_space=pltpu.VMEM)
    hbm = pl.BlockSpec(memory_space=pltpu.HBM)
    dma = pltpu.SemaphoreType.DMA
    list_len = locals_ * slots
    line = pltpu.VMEM((CHUNKS, last, slots, cw), BF16)
    plane = pltpu.VMEM((CHUNKS, nodes, TILE, bw), BF16)
    stacked = BLOCKS * slots
    rows, gradient = pl.pallas_call(
        functools.partial(kernel, nodes, locals_, cap),
        out_shape=(
            jax.ShapeDtypeStruct((list_len, width), BF16),
            jax.ShapeDtypeStruct((touch, width), F32),
        ),
        in_specs=[vmem] * 4 + [hbm] * 4,
        out_specs=[vmem] * 2,
        scratch_shapes=[
            pltpu.VMEM((tokens, width), BF16),
            pltpu.VMEM((touch, width), F32),
            pltpu.VMEM((touch, width), F32),
            pltpu.VMEM((touch, width), F32),
            pltpu.VMEM((nodes * TILE, stacked), BF16),
            pltpu.VMEM((stacked, nodes * TILE), BF16),
            pltpu.VMEM((BLOCKS * touch, nodes * TILE), BF16),
            pltpu.VMEM((nodes * TILE, BLOCKS * touch), BF16),
            pltpu.VMEM((list_len, tokens), BF16),
            pltpu.VMEM((CHUNKS, locals_, slots, cw), F32),
            line,
            line,
            line,
            line,
            plane,
            plane,
            plane,
            plane,
            dma((CHUNKS,)),
            dma((3,)),
            dma((CHUNKS, last)),
            dma((CHUNKS, last)),
            dma((CHUNKS, last)),
            dma((CHUNKS, last)),
            dma((CHUNKS,)),
            dma((CHUNKS,)),
            dma((CHUNKS,)),
            dma((CHUNKS,)),
            dma((CHUNKS, locals_)),
            dma((CHUNKS, locals_)),
            dma((CHUNKS, locals_)),
        ],
        compiler_params=pltpu.CompilerParams(
            collective_id=0, has_side_effects=True, vmem_limit_bytes=44 * 1024 * 1024
        ),
    )(
        token_slot.reshape(1, tokens),
        node_ids,
        touched_ids.reshape(1, touch),
        jnp.swapaxes(owner_map, 1, 2).reshape(cap, nodes),
        grads,
        moment,
        second,
        master,
    )
    moment_out, second_out, master_out = adam_rows(
        gradient, moment, second, master, touched_ids[:, None] >= 0
    )
    wanted = lax.iota(jnp.int32, list_len)
    selector = (token_slot[:, None] == wanted[None, :]).astype(BF16)
    return dot(selector, rows).astype(BF16), moment_out, second_out, master_out


def solution(mesh):
    nodes, locals_ = mesh.shape["node"], mesh.shape["local"]
    placed = (
        P(("node", "local"), None),
        P(("node", "local")),
        P("node", "local"),
        P(("node", "local")),
        P(("node", "local"), None, None),
        P(("node", "local"), None),
        P(("node", "local"), None),
        P(("node", "local"), None),
    )
    return jax.shard_map(
        functools.partial(on_device, nodes, locals_),
        mesh=mesh,
        in_specs=placed,
        out_specs=(P(("node", "local"), None),) * 4,
        check_vma=False,
    )
```

```python
import functools

import jax
import jax.numpy as jnp
from jax import lax
from jax.experimental import pallas as pl
from jax.experimental.pallas import tpu as pltpu
from jax.sharding import PartitionSpec as P

VOCAB = 262144
STEP = 100

BETA_ONE = 0.9
BETA_TWO = 0.999
LEARN_RATE = 0.01
EPSILON = 1e-08

MESH = pl.DeviceIdType.MESH
CHUNKS = 3
BLOCKS = 7
TILE = 16
F32 = jnp.float32
BF16 = jnp.bfloat16


def adam_rows(gradient, moment, second, master, kept):
    corr_one = 1.0 - BETA_ONE**STEP
    corr_two = 1.0 - BETA_TWO**STEP
    moment_new = BETA_ONE * moment + (1.0 - BETA_ONE) * gradient
    second_new = BETA_TWO * second + (1.0 - BETA_TWO) * gradient * gradient
    master_new = master - LEARN_RATE * (moment_new / corr_one) / (
        jnp.sqrt(second_new / corr_two) + EPSILON
    )
    return (
        jnp.where(kept, moment_new, moment),
        jnp.where(kept, second_new, second),
        jnp.where(kept, master_new, master),
    )


def repeat(count, body):
    if count <= 8:
        for step in range(count):
            body(step)
    else:
        lax.fori_loop(0, count, lambda step, carry: (body(step), carry)[1], None)


def div(x, m):
    return lax.shift_right_logical(x, m.bit_length() - 1) if m & (m - 1) == 0 else x // m


def mod(x, m):
    return x & (m - 1) if m & (m - 1) == 0 else x % m


def dot(a, b):
    return jnp.dot(a, b, preferred_element_type=F32)


def kernel(
    nodes,
    locals_,
    cap,
    slot_ref,
    ids_ref,
    touched_ref,
    omap_ref,
    grads_hbm,
    moment_hbm,
    second_hbm,
    master_hbm,
    gath,
    gradient_out,
    grads,
    moment,
    second,
    master,
    route,
    route_t,
    collect,
    collect_t,
    select,
    part,
    up_src,
    up_dst,
    dn_src,
    dn_dst,
    fwd_src,
    fwd_dst,
    rep_src,
    rep_dst,
    load_sem,
    adam_sem,
    up_ss,
    up_rs,
    dn_ss,
    dn_rs,
    fwd_ss,
    fwd_rs,
    rep_ss,
    rep_rs,
    ag_up_ss,
    ag_dn_ss,
    ag_rs,
):
    n = lax.axis_index("node")
    j = lax.axis_index("local")
    last = locals_ - 1
    half = locals_ // 2
    width = grads.shape[1]
    cw = width // CHUNKS
    bw = cw // BLOCKS
    slots = part.shape[2]
    group = TILE // cap
    stacked = BLOCKS * slots

    loads = []
    for k in range(CHUNKS):
        cols = pl.ds(k * cw, cw)
        loads.append(
            pltpu.make_async_copy(grads_hbm.at[:, cols], grads.at[:, cols], load_sem.at[k])
        )
        loads[-1].start()
    adam_loads = [
        pltpu.make_async_copy(src, dst, adam_sem.at[i])
        for i, (src, dst) in enumerate(
            ((moment_hbm, moment), (second_hbm, second), (master_hbm, master))
        )
    ]
    for copy in adam_loads:
        copy.start()

    barrier = pltpu.get_barrier_semaphore()

    def greet(p):
        pl.semaphore_signal(
            barrier, inc=1, device_id=(lax.rem(n + p + 1, nodes), j), device_id_type=MESH
        )

    def greet_line(peer):
        pl.semaphore_signal(barrier, inc=1, device_id=(n, peer), device_id_type=MESH)

    tree = locals_ == 4
    inner = jnp.clip(j, 1, 2)
    outer = 3 * (inner - 1)
    far_inner, far_outer = 3 - inner, 3 - outer
    partner = inner + outer - j
    is_inner = j == inner
    if tree:
        greet_line(partner)
        greet_line(far_inner)
        pl.when(is_inner)(lambda: greet_line(far_outer))
        line_peers = 2 + jnp.minimum(j, 1) * jnp.minimum(last - j, 1)
    else:
        pl.when(j > 0)(lambda: greet_line(j - 1))
        pl.when(j < last)(lambda: greet_line(j + 1))
        line_peers = jnp.minimum(j, 1) + jnp.minimum(last - j, 1)
    repeat(nodes - 1, greet)

    def iota(shape, dim):
        return lax.broadcasted_iota(jnp.int32, shape, dim)

    def column(row, size):
        diagonal = iota((size, size), 0) == iota((size, size), 1)
        return jnp.sum(jnp.where(diagonal, row, 0.0), axis=1, keepdims=True)

    shape = select.shape
    select[...] = jnp.where(iota(shape, 0) == slot_ref[...], 1.0, 0.0).astype(BF16)

    pl.semaphore_wait(barrier, nodes - 1 + line_peers)

    def up_copy(k, s):
        return pltpu.make_async_remote_copy(
            up_src.at[k, s],
            up_dst.at[k, s],
            up_ss.at[k, s],
            up_rs.at[k, s],
            device_id=(n, jnp.minimum(j + 1, last)),
            device_id_type=MESH,
        )

    def dn_copy(k, s):
        return pltpu.make_async_remote_copy(
            dn_src.at[k, s],
            dn_dst.at[k, s],
            dn_ss.at[k, s],
            dn_rs.at[k, s],
            device_id=(n, jnp.maximum(j - 1, 0)),
            device_id_type=MESH,
        )

    def ag_copy(k, t, up):
        rows = gath.at[pl.ds(pl.multiple_of(t * slots, slots), slots), pl.ds(k * cw, cw)]
        return pltpu.make_async_remote_copy(
            rows,
            rows,
            (ag_up_ss if up else ag_dn_ss).at[k, t],
            ag_rs.at[k, t],
            device_id=(n, jnp.minimum(j + 1, last) if up else jnp.maximum(j - 1, 0)),
            device_id_type=MESH,
        )

    def send_nodes(k, src, dst, ss, rs):
        def send(p):
            peer = lax.rem(n + p + 1, nodes)
            pltpu.make_async_remote_copy(
                src.at[k, peer],
                dst.at[k, n],
                ss.at[k],
                rs.at[k],
                device_id=(peer, j),
                device_id_type=MESH,
            ).start()

        repeat(nodes - 1, send)
        dst[k, n] = src[k, n]

    def wait_nodes(k, buf, sem):
        whole = buf.at[k, pl.ds(0, nodes - 1)]
        pltpu.make_async_copy(whole, whole, sem.at[k]).wait()

    def sums(k):
        loads[k].wait()
        total = dot(select[...], grads[:, k * cw : (k + 1) * cw])
        part[k] = total.reshape(locals_, slots, cw)

    def begin(k):
        sums(k)

        @pl.when(j == 0)
        def _():
            def step(s):
                up_src[k, s] = part[k, last - s].astype(BF16)
                up_copy(k, s).start()

            repeat(last, step)

        @pl.when(j == last)
        def _():
            def step(s):
                dn_src[k, s] = part[k, s].astype(BF16)
                dn_copy(k, s).start()

            repeat(last, step)

    def up_relay(k):
        def step(s):
            @pl.when(last - s > j)
            def _():
                up_copy(k, s).wait_recv()
                up_src[k, s] = (up_dst[k, s].astype(F32) + part[k, last - s]).astype(BF16)
                up_copy(k, s).start()

        repeat(last, step)

    def dn_relay(k):
        def step(s):
            @pl.when(s < j)
            def _():
                dn_copy(k, s).wait_recv()
                dn_src[k, s] = (dn_dst[k, s].astype(F32) + part[k, s]).astype(BF16)
                dn_copy(k, s).start()

        repeat(last, step)

    def near(k):
        pl.when((j > 0) & (j < half))(lambda: up_relay(k))
        pl.when((j < last) & (j >= half))(lambda: dn_relay(k))

    def far(k):
        pl.when((j > 0) & (j < half))(lambda: dn_relay(k))
        pl.when((j < last) & (j >= half))(lambda: up_relay(k))

    def forward(k):
        @pl.when(j > 0)
        def _():
            up_copy(k, last - j).wait_recv()
            part[k, j] = part[k, j] + up_dst[k, last - j].astype(F32)

        @pl.when(j < last)
        def _():
            dn_copy(k, j).wait_recv()
            part[k, j] = part[k, j] + dn_dst[k, j].astype(F32)

        send_out(k, part[k, j])

    def send_out(k, total):
        own = total.astype(BF16)
        tall = jnp.concatenate([own[:, b * bw : (b + 1) * bw] for b in range(BLOCKS)], axis=0)
        fwd_src[k] = dot(route[...], tall).astype(BF16).reshape(nodes, TILE, bw)
        send_nodes(k, fwd_src, fwd_dst, fwd_ss, fwd_rs)

    def update(k):
        if k == 0:
            for copy in adam_loads:
                copy.wait()
        wait_nodes(k, fwd_dst, fwd_rs)
        gradient = dot(collect[...], fwd_dst[k].reshape(nodes * TILE, bw))
        fresh = []
        for b in range(BLOCKS):
            cols = slice(k * cw + b * bw, k * cw + (b + 1) * bw)
            new = adam_rows(
                gradient[b * TILE : (b + 1) * TILE],
                moment[:, cols],
                second[:, cols],
                master[:, cols],
                kept,
            )
            gradient_out[:, cols] = gradient[b * TILE : (b + 1) * TILE]
            fresh.append(new[2].astype(BF16))
        tall = jnp.concatenate(fresh, axis=0)
        rep_src[k] = dot(collect_t[...], tall).astype(BF16).reshape(nodes, TILE, bw)
        send_nodes(k, rep_src, rep_dst, rep_ss, rep_rs)

    def fill(k):
        wait_nodes(k, rep_dst, rep_rs)
        rows = dot(route_t[...], rep_dst[k].reshape(nodes * TILE, bw)).astype(BF16)
        own = pl.ds(pl.multiple_of(j * slots, slots), slots)
        for b in range(BLOCKS):
            cols = slice(k * cw + b * bw, k * cw + (b + 1) * bw)
            gath[own, cols] = rows[b * slots : (b + 1) * slots]

    def listed(k):
        fill(k)

        @pl.when(j < last)
        def _():
            ag_copy(k, j, True).start()

        @pl.when(j > 0)
        def _():
            ag_copy(k, j, False).start()

    def pass_on(k, d):
        low, high = j - 1 - d, j + 1 + d

        @pl.when(low >= 0)
        def _():
            ag_copy(k, low, True).wait_recv()

            @pl.when(j < last)
            def _():
                ag_copy(k, low, True).start()

        @pl.when(high <= last)
        def _():
            ag_copy(k, high, False).wait_recv()

            @pl.when(j > 0)
            def _():
                ag_copy(k, high, False).start()

    def first_hop(k):
        pass_on(k, 0)

    def middle_hops(k):
        repeat(last - 2, lambda d: pass_on(k, d + 1))

    def last_hop(k):
        pass_on(k, last - 1)

    def pair_copy(k):
        rows = pl.ds(0, 2)
        return pltpu.make_async_remote_copy(
            up_src.at[k, rows],
            up_dst.at[k, rows],
            up_ss.at[k, 0],
            up_rs.at[k, 0],
            device_id=(n, partner),
            device_id_type=MESH,
        )

    def partner_copy(k):
        return pltpu.make_async_remote_copy(
            up_src.at[k, 2],
            up_dst.at[k, 2],
            up_ss.at[k, 2],
            up_rs.at[k, 1],
            device_id=(n, partner),
            device_id_type=MESH,
        )

    def far_copy(k, i):
        return pltpu.make_async_remote_copy(
            up_src.at[k, i],
            dn_dst.at[k, 0],
            up_ss.at[k, i],
            up_rs.at[k, 2],
            device_id=(n, far_outer if i else far_inner),
            device_id_type=MESH,
        )

    def row_copy(k, t, peer, i):
        rows = gath.at[pl.ds(pl.multiple_of(t * slots, slots), slots), pl.ds(k * cw, cw)]
        return pltpu.make_async_remote_copy(
            rows,
            rows,
            ag_up_ss.at[k, i],
            ag_rs.at[k, t],
            device_id=(n, peer),
            device_id_type=MESH,
        )

    def tree_begin(k):
        sums(k)

        @pl.when(~is_inner)
        def _():
            up_src[k, 0] = part[k, far_inner].astype(BF16)
            up_src[k, 1] = part[k, far_outer].astype(BF16)
            pair_copy(k).start()

        up_src[k, 2] = part[k, partner].astype(BF16)
        partner_copy(k).start()

    def merge(k):
        @pl.when(is_inner)
        def _():
            pair_copy(k).wait_recv()
            for i, t in enumerate((far_inner, far_outer)):
                up_src[k, i] = (up_dst[k, i].astype(F32) + part[k, t]).astype(BF16)
                far_copy(k, i).start()

    def tree_forward(k):
        partner_copy(k).wait_recv()
        far_copy(k, 0).wait_recv()
        send_out(k, part[k, j] + up_dst[k, 2].astype(F32) + dn_dst[k, 0].astype(F32))

    def tree_listed(k):
        fill(k)
        row_copy(k, j, far_inner, 0).start()
        row_copy(k, j, partner, 1).start()

    def tree_pass(k):
        @pl.when(is_inner)
        def _():
            for i, t in enumerate((far_inner, far_outer)):
                row_copy(k, t, partner, 2 + i).wait_recv()
                row_copy(k, t, partner, 2 + i).start()

    def tree_last(k):
        row_copy(k, partner, partner, 1).wait_recv()

        @pl.when(~is_inner)
        def _():
            for t in (far_inner, far_outer):
                row_copy(k, t, partner, 0).wait_recv()

    def tree_drain(k):
        @pl.when(is_inner)
        def _():
            for i in range(2):
                far_copy(k, i).wait_send()
                row_copy(k, far_outer if i else far_inner, partner, 2 + i).wait_send()

        @pl.when(~is_inner)
        def _():
            pair_copy(k).wait_send()

        partner_copy(k).wait_send()
        row_copy(k, j, far_inner, 0).wait_send()
        row_copy(k, j, partner, 1).wait_send()

    for k in range(CHUNKS):
        tree_begin(k) if tree else begin(k)

    rows_node = VOCAB // nodes
    owner = lax.shift_right_logical(ids_ref[...], rows_node.bit_length() - 1).astype(F32)
    shape = (slots, slots)
    earlier = (column(owner, slots) == owner) & (iota(shape, 0) < iota(shape, 1))
    rank = jnp.sum(jnp.where(earlier, 1.0, 0.0), axis=0, keepdims=True)
    sent = column(owner * float(cap) + rank, slots)
    shape = (slots, stacked)
    sent = jnp.sum(
        jnp.where(iota(shape, 0) == mod(iota(shape, 1), slots), sent, 0.0), axis=0, keepdims=True
    )
    shape = route.shape
    sub, lane = iota(shape, 0), iota(shape, 1)
    wanted = (div(sub, TILE) * cap + div(mod(sub, TILE), group)).astype(F32)
    routed = jnp.where((wanted == sent) & (mod(sub, group) == div(lane, slots)), 1.0, 0.0).astype(F32)
    route[...] = routed.astype(BF16)

    shape = (nodes, nodes * TILE)
    sub, lane = iota(shape, 0), iota(shape, 1)
    place = jnp.zeros((1, nodes * TILE), F32)
    for c in range(cap):
        held = column(omap_ref[c : c + 1, :].astype(F32), nodes)
        here = (sub == div(lane, TILE)) & (div(mod(lane, TILE), group) == c)
        place = place + jnp.sum(jnp.where(here, held, 0.0), axis=0, keepdims=True)
    shape = collect.shape
    sub, lane = iota(shape, 0), iota(shape, 1)
    taken = jnp.where(
        (mod(sub, TILE).astype(F32) == place) & (div(sub, TILE) == mod(lane, group)), 1.0, 0.0
    ).astype(F32)
    collect[...] = taken.astype(BF16)

    route_t[...] = routed.T.astype(BF16)
    collect_t[...] = taken.T.astype(BF16)
    kept = column(touched_ref[...].astype(F32), touched_ref.shape[1]) >= 0.0

    if tree:
        stages = (merge, tree_forward, update, tree_listed, tree_pass, tree_last)
    else:
        stages = (near, far, forward, update, listed, first_hop, middle_hops, last_hop)
    for tick in range(CHUNKS + len(stages) - 1):
        for depth in reversed(range(len(stages))):
            if 0 <= tick - depth < CHUNKS:
                stages[depth](tick - depth)

    for k in range(CHUNKS):
        wait_nodes(k, fwd_src, fwd_ss)
        wait_nodes(k, rep_src, rep_ss)
        if tree:
            tree_drain(k)
            continue

        def drain(s):
            @pl.when(last - s > j)
            def _():
                up_copy(k, s).wait_send()

            @pl.when(s < j)
            def _():
                dn_copy(k, s).wait_send()

        repeat(last, drain)

        def drain_gather(t):
            @pl.when((t <= j) & (j < last))
            def _():
                ag_copy(k, t, True).wait_send()

            @pl.when((t >= j) & (j > 0))
            def _():
                ag_copy(k, t, False).wait_send()

        repeat(locals_, drain_gather)


def on_device(nodes, locals_, grads, token_slot, node_ids, touched_ids, owner_map, moment, second, master):
    tokens, width = grads.shape
    slots = node_ids.shape[1]
    touch = touched_ids.shape[0]
    cap = owner_map.shape[2]
    group = TILE // cap
    cw = width // CHUNKS
    bw = cw // BLOCKS
    last = locals_ - 1
    vmem = pl.BlockSpec(memory_space=pltpu.VMEM)
    hbm = pl.BlockSpec(memory_space=pltpu.HBM)
    dma = pltpu.SemaphoreType.DMA
    list_len = locals_ * slots
    line = pltpu.VMEM((CHUNKS, last, slots, cw), BF16)
    plane = pltpu.VMEM((CHUNKS, nodes, TILE, bw), BF16)
    stacked = BLOCKS * slots
    rows, gradient = pl.pallas_call(
        functools.partial(kernel, nodes, locals_, cap),
        out_shape=(
            jax.ShapeDtypeStruct((list_len, width), BF16),
            jax.ShapeDtypeStruct((touch, width), F32),
        ),
        in_specs=[vmem] * 4 + [hbm] * 4,
        out_specs=[vmem] * 2,
        scratch_shapes=[
            pltpu.VMEM((tokens, width), BF16),
            pltpu.VMEM((touch, width), F32),
            pltpu.VMEM((touch, width), F32),
            pltpu.VMEM((touch, width), F32),
            pltpu.VMEM((nodes * TILE, stacked), BF16),
            pltpu.VMEM((stacked, nodes * TILE), BF16),
            pltpu.VMEM((BLOCKS * touch, nodes * TILE), BF16),
            pltpu.VMEM((nodes * TILE, BLOCKS * touch), BF16),
            pltpu.VMEM((list_len, tokens), BF16),
            pltpu.VMEM((CHUNKS, locals_, slots, cw), F32),
            line,
            line,
            line,
            line,
            plane,
            plane,
            plane,
            plane,
            dma((CHUNKS,)),
            dma((3,)),
            dma((CHUNKS, last)),
            dma((CHUNKS, last)),
            dma((CHUNKS, last)),
            dma((CHUNKS, last)),
            dma((CHUNKS,)),
            dma((CHUNKS,)),
            dma((CHUNKS,)),
            dma((CHUNKS,)),
            dma((CHUNKS, locals_)),
            dma((CHUNKS, locals_)),
            dma((CHUNKS, locals_)),
        ],
        compiler_params=pltpu.CompilerParams(
            collective_id=0, has_side_effects=True, vmem_limit_bytes=56 * 1024 * 1024
        ),
    )(
        token_slot.reshape(1, tokens),
        node_ids,
        touched_ids.reshape(1, touch),
        jnp.swapaxes(owner_map, 1, 2).reshape(cap, nodes),
        grads,
        moment,
        second,
        master,
    )
    moment_out, second_out, master_out = adam_rows(
        gradient, moment, second, master, touched_ids[:, None] >= 0
    )
    wanted = lax.iota(jnp.int32, list_len)
    selector = (token_slot[:, None] == wanted[None, :]).astype(BF16)
    return dot(selector, rows).astype(BF16), moment_out, second_out, master_out


def solution(mesh):
    nodes, locals_ = mesh.shape["node"], mesh.shape["local"]
    placed = (
        P(("node", "local"), None),
        P(("node", "local")),
        P("node", "local"),
        P(("node", "local")),
        P(("node", "local"), None, None),
        P(("node", "local"), None),
        P(("node", "local"), None),
        P(("node", "local"), None),
    )
    return jax.shard_map(
        functools.partial(on_device, nodes, locals_),
        mesh=mesh,
        in_specs=placed,
        out_specs=(P(("node", "local"), None),) * 4,
        check_vma=False,
    )
```

```python
import functools

import jax
import jax.numpy as jnp
from jax import lax
from jax.experimental import pallas as pl
from jax.experimental.pallas import tpu as pltpu
from jax.sharding import PartitionSpec as P

VOCAB = 262144
STEP = 100

BETA_ONE = 0.9
BETA_TWO = 0.999
LEARN_RATE = 0.01
EPSILON = 1e-08

MESH = pl.DeviceIdType.MESH
CHUNKS = 6
BLOCKS = 7
TILE = 16
F32 = jnp.float32
BF16 = jnp.bfloat16


def adam_rows(gradient, moment, second, master, kept):
    corr_one = 1.0 - BETA_ONE**STEP
    corr_two = 1.0 - BETA_TWO**STEP
    moment_new = BETA_ONE * moment + (1.0 - BETA_ONE) * gradient
    second_new = BETA_TWO * second + (1.0 - BETA_TWO) * gradient * gradient
    master_new = master - LEARN_RATE * (moment_new / corr_one) / (
        jnp.sqrt(second_new / corr_two) + EPSILON
    )
    return (
        jnp.where(kept, moment_new, moment),
        jnp.where(kept, second_new, second),
        jnp.where(kept, master_new, master),
    )


def repeat(count, body):
    if count <= 8:
        for step in range(count):
            body(step)
    else:
        lax.fori_loop(0, count, lambda step, carry: (body(step), carry)[1], None)


def div(x, m):
    return lax.shift_right_logical(x, m.bit_length() - 1) if m & (m - 1) == 0 else x // m


def mod(x, m):
    return x & (m - 1) if m & (m - 1) == 0 else x % m


def dot(a, b):
    return jnp.dot(a, b, preferred_element_type=F32)


def kernel(
    nodes,
    locals_,
    cap,
    slot_ref,
    ids_ref,
    touched_ref,
    omap_ref,
    grads_hbm,
    moment_hbm,
    second_hbm,
    master_hbm,
    gath,
    gradient_out,
    grads,
    moment,
    second,
    master,
    route,
    route_t,
    collect,
    collect_t,
    select,
    part,
    up_src,
    up_dst,
    dn_src,
    dn_dst,
    fwd_src,
    fwd_dst,
    rep_src,
    rep_dst,
    load_sem,
    adam_sem,
    up_ss,
    up_rs,
    dn_ss,
    dn_rs,
    fwd_ss,
    fwd_rs,
    rep_ss,
    rep_rs,
    ag_up_ss,
    ag_dn_ss,
    ag_rs,
):
    n = lax.axis_index("node")
    j = lax.axis_index("local")
    last = locals_ - 1
    half = locals_ // 2
    width = grads.shape[1]
    cw = width // CHUNKS
    bw = cw // BLOCKS
    slots = part.shape[2]
    group = TILE // cap
    stacked = BLOCKS * slots

    loads = []
    for k in range(CHUNKS):
        cols = pl.ds(k * cw, cw)
        loads.append(
            pltpu.make_async_copy(grads_hbm.at[:, cols], grads.at[:, cols], load_sem.at[k])
        )
        loads[-1].start()
    adam_loads = [
        pltpu.make_async_copy(src, dst, adam_sem.at[i])
        for i, (src, dst) in enumerate(
            ((moment_hbm, moment), (second_hbm, second), (master_hbm, master))
        )
    ]
    for copy in adam_loads:
        copy.start()

    barrier = pltpu.get_barrier_semaphore()

    def greet(p):
        pl.semaphore_signal(
            barrier, inc=1, device_id=(lax.rem(n + p + 1, nodes), j), device_id_type=MESH
        )

    def greet_line(peer):
        pl.semaphore_signal(barrier, inc=1, device_id=(n, peer), device_id_type=MESH)

    tree = locals_ == 4
    inner = jnp.clip(j, 1, 2)
    outer = 3 * (inner - 1)
    far_inner, far_outer = 3 - inner, 3 - outer
    partner = inner + outer - j
    is_inner = j == inner
    if tree:
        greet_line(partner)
        greet_line(far_inner)
        pl.when(is_inner)(lambda: greet_line(far_outer))
        line_peers = 2 + jnp.minimum(j, 1) * jnp.minimum(last - j, 1)
    else:
        pl.when(j > 0)(lambda: greet_line(j - 1))
        pl.when(j < last)(lambda: greet_line(j + 1))
        line_peers = jnp.minimum(j, 1) + jnp.minimum(last - j, 1)
    repeat(nodes - 1, greet)

    def iota(shape, dim):
        return lax.broadcasted_iota(jnp.int32, shape, dim)

    def column(row, size):
        diagonal = iota((size, size), 0) == iota((size, size), 1)
        return jnp.sum(jnp.where(diagonal, row, 0.0), axis=1, keepdims=True)

    shape = select.shape
    select[...] = jnp.where(iota(shape, 0) == slot_ref[...], 1.0, 0.0).astype(BF16)

    pl.semaphore_wait(barrier, nodes - 1 + line_peers)

    def up_copy(k, s):
        return pltpu.make_async_remote_copy(
            up_src.at[k, s],
            up_dst.at[k, s],
            up_ss.at[k, s],
            up_rs.at[k, s],
            device_id=(n, jnp.minimum(j + 1, last)),
            device_id_type=MESH,
        )

    def dn_copy(k, s):
        return pltpu.make_async_remote_copy(
            dn_src.at[k, s],
            dn_dst.at[k, s],
            dn_ss.at[k, s],
            dn_rs.at[k, s],
            device_id=(n, jnp.maximum(j - 1, 0)),
            device_id_type=MESH,
        )

    def ag_copy(k, t, up):
        rows = gath.at[pl.ds(pl.multiple_of(t * slots, slots), slots), pl.ds(k * cw, cw)]
        return pltpu.make_async_remote_copy(
            rows,
            rows,
            (ag_up_ss if up else ag_dn_ss).at[k, t],
            ag_rs.at[k, t],
            device_id=(n, jnp.minimum(j + 1, last) if up else jnp.maximum(j - 1, 0)),
            device_id_type=MESH,
        )

    def send_nodes(k, src, dst, ss, rs):
        def send(p):
            peer = lax.rem(n + p + 1, nodes)
            pltpu.make_async_remote_copy(
                src.at[k, peer],
                dst.at[k, n],
                ss.at[k],
                rs.at[k],
                device_id=(peer, j),
                device_id_type=MESH,
            ).start()

        repeat(nodes - 1, send)
        dst[k, n] = src[k, n]

    def wait_nodes(k, buf, sem):
        whole = buf.at[k, pl.ds(0, nodes - 1)]
        pltpu.make_async_copy(whole, whole, sem.at[k]).wait()

    def sums(k):
        loads[k].wait()
        total = dot(select[...], grads[:, k * cw : (k + 1) * cw])
        part[k] = total.reshape(locals_, slots, cw)

    def begin(k):
        sums(k)

        @pl.when(j == 0)
        def _():
            def step(s):
                up_src[k, s] = part[k, last - s].astype(BF16)
                up_copy(k, s).start()

            repeat(last, step)

        @pl.when(j == last)
        def _():
            def step(s):
                dn_src[k, s] = part[k, s].astype(BF16)
                dn_copy(k, s).start()

            repeat(last, step)

    def up_relay(k):
        def step(s):
            @pl.when(last - s > j)
            def _():
                up_copy(k, s).wait_recv()
                up_src[k, s] = (up_dst[k, s].astype(F32) + part[k, last - s]).astype(BF16)
                up_copy(k, s).start()

        repeat(last, step)

    def dn_relay(k):
        def step(s):
            @pl.when(s < j)
            def _():
                dn_copy(k, s).wait_recv()
                dn_src[k, s] = (dn_dst[k, s].astype(F32) + part[k, s]).astype(BF16)
                dn_copy(k, s).start()

        repeat(last, step)

    def near(k):
        pl.when((j > 0) & (j < half))(lambda: up_relay(k))
        pl.when((j < last) & (j >= half))(lambda: dn_relay(k))

    def far(k):
        pl.when((j > 0) & (j < half))(lambda: dn_relay(k))
        pl.when((j < last) & (j >= half))(lambda: up_relay(k))

    def forward(k):
        @pl.when(j > 0)
        def _():
            up_copy(k, last - j).wait_recv()
            part[k, j] = part[k, j] + up_dst[k, last - j].astype(F32)

        @pl.when(j < last)
        def _():
            dn_copy(k, j).wait_recv()
            part[k, j] = part[k, j] + dn_dst[k, j].astype(F32)

        send_out(k, part[k, j])

    def send_out(k, total):
        own = total.astype(BF16)
        tall = jnp.concatenate([own[:, b * bw : (b + 1) * bw] for b in range(BLOCKS)], axis=0)
        fwd_src[k] = dot(route[...], tall).astype(BF16).reshape(nodes, TILE, bw)
        send_nodes(k, fwd_src, fwd_dst, fwd_ss, fwd_rs)

    def update(k):
        if k == 0:
            for copy in adam_loads:
                copy.wait()
        wait_nodes(k, fwd_dst, fwd_rs)
        gradient = dot(collect[...], fwd_dst[k].reshape(nodes * TILE, bw))
        fresh = []
        for b in range(BLOCKS):
            cols = slice(k * cw + b * bw, k * cw + (b + 1) * bw)
            new = adam_rows(
                gradient[b * TILE : (b + 1) * TILE],
                moment[:, cols],
                second[:, cols],
                master[:, cols],
                kept,
            )
            gradient_out[:, cols] = gradient[b * TILE : (b + 1) * TILE]
            fresh.append(new[2].astype(BF16))
        tall = jnp.concatenate(fresh, axis=0)
        rep_src[k] = dot(collect_t[...], tall).astype(BF16).reshape(nodes, TILE, bw)
        send_nodes(k, rep_src, rep_dst, rep_ss, rep_rs)

    def fill(k):
        wait_nodes(k, rep_dst, rep_rs)
        rows = dot(route_t[...], rep_dst[k].reshape(nodes * TILE, bw)).astype(BF16)
        own = pl.ds(pl.multiple_of(j * slots, slots), slots)
        for b in range(BLOCKS):
            cols = slice(k * cw + b * bw, k * cw + (b + 1) * bw)
            gath[own, cols] = rows[b * slots : (b + 1) * slots]

    def listed(k):
        fill(k)

        @pl.when(j < last)
        def _():
            ag_copy(k, j, True).start()

        @pl.when(j > 0)
        def _():
            ag_copy(k, j, False).start()

    def pass_on(k, d):
        low, high = j - 1 - d, j + 1 + d

        @pl.when(low >= 0)
        def _():
            ag_copy(k, low, True).wait_recv()

            @pl.when(j < last)
            def _():
                ag_copy(k, low, True).start()

        @pl.when(high <= last)
        def _():
            ag_copy(k, high, False).wait_recv()

            @pl.when(j > 0)
            def _():
                ag_copy(k, high, False).start()

    def first_hop(k):
        pass_on(k, 0)

    def middle_hops(k):
        repeat(last - 2, lambda d: pass_on(k, d + 1))

    def last_hop(k):
        pass_on(k, last - 1)

    def pair_copy(k):
        rows = pl.ds(0, 2)
        return pltpu.make_async_remote_copy(
            up_src.at[k, rows],
            up_dst.at[k, rows],
            up_ss.at[k, 0],
            up_rs.at[k, 0],
            device_id=(n, partner),
            device_id_type=MESH,
        )

    def partner_copy(k):
        return pltpu.make_async_remote_copy(
            up_src.at[k, 2],
            up_dst.at[k, 2],
            up_ss.at[k, 2],
            up_rs.at[k, 1],
            device_id=(n, partner),
            device_id_type=MESH,
        )

    def far_copy(k, i):
        return pltpu.make_async_remote_copy(
            up_src.at[k, i],
            dn_dst.at[k, 0],
            up_ss.at[k, i],
            up_rs.at[k, 2],
            device_id=(n, far_outer if i else far_inner),
            device_id_type=MESH,
        )

    def row_copy(k, t, peer, i):
        rows = gath.at[pl.ds(pl.multiple_of(t * slots, slots), slots), pl.ds(k * cw, cw)]
        return pltpu.make_async_remote_copy(
            rows,
            rows,
            ag_up_ss.at[k, i],
            ag_rs.at[k, t],
            device_id=(n, peer),
            device_id_type=MESH,
        )

    def tree_begin(k):
        sums(k)

        @pl.when(~is_inner)
        def _():
            up_src[k, 0] = part[k, far_inner].astype(BF16)
            up_src[k, 1] = part[k, far_outer].astype(BF16)
            pair_copy(k).start()

        up_src[k, 2] = part[k, partner].astype(BF16)
        partner_copy(k).start()

    def merge(k):
        @pl.when(is_inner)
        def _():
            pair_copy(k).wait_recv()
            for i, t in enumerate((far_inner, far_outer)):
                up_src[k, i] = (up_dst[k, i].astype(F32) + part[k, t]).astype(BF16)
                far_copy(k, i).start()

    def tree_forward(k):
        partner_copy(k).wait_recv()
        far_copy(k, 0).wait_recv()
        send_out(k, part[k, j] + up_dst[k, 2].astype(F32) + dn_dst[k, 0].astype(F32))

    def tree_listed(k):
        fill(k)
        row_copy(k, j, far_inner, 0).start()
        row_copy(k, j, partner, 1).start()

    def tree_pass(k):
        @pl.when(is_inner)
        def _():
            for i, t in enumerate((far_inner, far_outer)):
                row_copy(k, t, partner, 2 + i).wait_recv()
                row_copy(k, t, partner, 2 + i).start()

    def tree_last(k):
        row_copy(k, partner, partner, 1).wait_recv()

        @pl.when(~is_inner)
        def _():
            for t in (far_inner, far_outer):
                row_copy(k, t, partner, 0).wait_recv()

    def tree_drain(k):
        @pl.when(is_inner)
        def _():
            for i in range(2):
                far_copy(k, i).wait_send()
                row_copy(k, far_outer if i else far_inner, partner, 2 + i).wait_send()

        @pl.when(~is_inner)
        def _():
            pair_copy(k).wait_send()

        partner_copy(k).wait_send()
        row_copy(k, j, far_inner, 0).wait_send()
        row_copy(k, j, partner, 1).wait_send()

    for k in range(CHUNKS):
        tree_begin(k) if tree else begin(k)

    rows_node = VOCAB // nodes
    owner = lax.shift_right_logical(ids_ref[...], rows_node.bit_length() - 1).astype(F32)
    shape = (slots, slots)
    earlier = (column(owner, slots) == owner) & (iota(shape, 0) < iota(shape, 1))
    rank = jnp.sum(jnp.where(earlier, 1.0, 0.0), axis=0, keepdims=True)
    sent = column(owner * float(cap) + rank, slots)
    shape = (slots, stacked)
    sent = jnp.sum(
        jnp.where(iota(shape, 0) == mod(iota(shape, 1), slots), sent, 0.0), axis=0, keepdims=True
    )
    shape = route.shape
    sub, lane = iota(shape, 0), iota(shape, 1)
    wanted = (div(sub, TILE) * cap + div(mod(sub, TILE), group)).astype(F32)
    routed = jnp.where((wanted == sent) & (mod(sub, group) == div(lane, slots)), 1.0, 0.0).astype(F32)
    route[...] = routed.astype(BF16)

    shape = (nodes, nodes * TILE)
    sub, lane = iota(shape, 0), iota(shape, 1)
    place = jnp.zeros((1, nodes * TILE), F32)
    for c in range(cap):
        held = column(omap_ref[c : c + 1, :].astype(F32), nodes)
        here = (sub == div(lane, TILE)) & (div(mod(lane, TILE), group) == c)
        place = place + jnp.sum(jnp.where(here, held, 0.0), axis=0, keepdims=True)
    shape = collect.shape
    sub, lane = iota(shape, 0), iota(shape, 1)
    taken = jnp.where(
        (mod(sub, TILE).astype(F32) == place) & (div(sub, TILE) == mod(lane, group)), 1.0, 0.0
    ).astype(F32)
    collect[...] = taken.astype(BF16)

    route_t[...] = routed.T.astype(BF16)
    collect_t[...] = taken.T.astype(BF16)
    kept = column(touched_ref[...].astype(F32), touched_ref.shape[1]) >= 0.0

    if tree:
        stages = (merge, tree_forward, update, tree_listed, tree_pass, tree_last)
    else:
        stages = (near, far, forward, update, listed, first_hop, middle_hops, last_hop)
    for tick in range(CHUNKS + len(stages) - 1):
        for depth in reversed(range(len(stages))):
            if 0 <= tick - depth < CHUNKS:
                stages[depth](tick - depth)

    for k in range(CHUNKS):
        wait_nodes(k, fwd_src, fwd_ss)
        wait_nodes(k, rep_src, rep_ss)
        if tree:
            tree_drain(k)
            continue

        def drain(s):
            @pl.when(last - s > j)
            def _():
                up_copy(k, s).wait_send()

            @pl.when(s < j)
            def _():
                dn_copy(k, s).wait_send()

        repeat(last, drain)

        def drain_gather(t):
            @pl.when((t <= j) & (j < last))
            def _():
                ag_copy(k, t, True).wait_send()

            @pl.when((t >= j) & (j > 0))
            def _():
                ag_copy(k, t, False).wait_send()

        repeat(locals_, drain_gather)


def on_device(nodes, locals_, grads, token_slot, node_ids, touched_ids, owner_map, moment, second, master):
    tokens, width = grads.shape
    slots = node_ids.shape[1]
    touch = touched_ids.shape[0]
    cap = owner_map.shape[2]
    group = TILE // cap
    cw = width // CHUNKS
    bw = cw // BLOCKS
    last = locals_ - 1
    vmem = pl.BlockSpec(memory_space=pltpu.VMEM)
    hbm = pl.BlockSpec(memory_space=pltpu.HBM)
    dma = pltpu.SemaphoreType.DMA
    list_len = locals_ * slots
    line = pltpu.VMEM((CHUNKS, last, slots, cw), BF16)
    plane = pltpu.VMEM((CHUNKS, nodes, TILE, bw), BF16)
    stacked = BLOCKS * slots
    rows, gradient = pl.pallas_call(
        functools.partial(kernel, nodes, locals_, cap),
        out_shape=(
            jax.ShapeDtypeStruct((list_len, width), BF16),
            jax.ShapeDtypeStruct((touch, width), F32),
        ),
        in_specs=[vmem] * 4 + [hbm] * 4,
        out_specs=[vmem] * 2,
        scratch_shapes=[
            pltpu.VMEM((tokens, width), BF16),
            pltpu.VMEM((touch, width), F32),
            pltpu.VMEM((touch, width), F32),
            pltpu.VMEM((touch, width), F32),
            pltpu.VMEM((nodes * TILE, stacked), BF16),
            pltpu.VMEM((stacked, nodes * TILE), BF16),
            pltpu.VMEM((BLOCKS * touch, nodes * TILE), BF16),
            pltpu.VMEM((nodes * TILE, BLOCKS * touch), BF16),
            pltpu.VMEM((list_len, tokens), BF16),
            pltpu.VMEM((CHUNKS, locals_, slots, cw), F32),
            line,
            line,
            line,
            line,
            plane,
            plane,
            plane,
            plane,
            dma((CHUNKS,)),
            dma((3,)),
            dma((CHUNKS, last)),
            dma((CHUNKS, last)),
            dma((CHUNKS, last)),
            dma((CHUNKS, last)),
            dma((CHUNKS,)),
            dma((CHUNKS,)),
            dma((CHUNKS,)),
            dma((CHUNKS,)),
            dma((CHUNKS, locals_)),
            dma((CHUNKS, locals_)),
            dma((CHUNKS, locals_)),
        ],
        compiler_params=pltpu.CompilerParams(
            collective_id=0, has_side_effects=True, vmem_limit_bytes=56 * 1024 * 1024
        ),
    )(
        token_slot.reshape(1, tokens),
        node_ids,
        touched_ids.reshape(1, touch),
        jnp.swapaxes(owner_map, 1, 2).reshape(cap, nodes),
        grads,
        moment,
        second,
        master,
    )
    moment_out, second_out, master_out = adam_rows(
        gradient, moment, second, master, touched_ids[:, None] >= 0
    )
    wanted = lax.iota(jnp.int32, list_len)
    selector = (token_slot[:, None] == wanted[None, :]).astype(BF16)
    return dot(selector, rows).astype(BF16), moment_out, second_out, master_out


def solution(mesh):
    nodes, locals_ = mesh.shape["node"], mesh.shape["local"]
    placed = (
        P(("node", "local"), None),
        P(("node", "local")),
        P("node", "local"),
        P(("node", "local")),
        P(("node", "local"), None, None),
        P(("node", "local"), None),
        P(("node", "local"), None),
        P(("node", "local"), None),
    )
    return jax.shard_map(
        functools.partial(on_device, nodes, locals_),
        mesh=mesh,
        in_specs=placed,
        out_specs=(P(("node", "local"), None),) * 4,
        check_vma=False,
    )
```

```python
import functools

import jax
import jax.numpy as jnp
from jax import lax
from jax.experimental import pallas as pl
from jax.experimental.pallas import tpu as pltpu
from jax.sharding import PartitionSpec as P

VOCAB = 262144
STEP = 100

BETA_ONE = 0.9
BETA_TWO = 0.999
LEARN_RATE = 0.01
EPSILON = 1e-08

MESH = pl.DeviceIdType.MESH
CHUNKS = 3
BLOCKS = 7
TILE = 16
F32 = jnp.float32
BF16 = jnp.bfloat16


def adam_rows(gradient, moment, second, master, kept):
    corr_one = 1.0 - BETA_ONE**STEP
    corr_two = 1.0 - BETA_TWO**STEP
    moment_new = BETA_ONE * moment + (1.0 - BETA_ONE) * gradient
    second_new = BETA_TWO * second + (1.0 - BETA_TWO) * gradient * gradient
    master_new = master - LEARN_RATE * (moment_new / corr_one) / (
        jnp.sqrt(second_new / corr_two) + EPSILON
    )
    return (
        jnp.where(kept, moment_new, moment),
        jnp.where(kept, second_new, second),
        jnp.where(kept, master_new, master),
    )


def repeat(count, body):
    if count <= 8:
        for step in range(count):
            body(step)
    else:
        lax.fori_loop(0, count, lambda step, carry: (body(step), carry)[1], None)


def div(x, m):
    return lax.shift_right_logical(x, m.bit_length() - 1) if m & (m - 1) == 0 else x // m


def mod(x, m):
    return x & (m - 1) if m & (m - 1) == 0 else x % m


def iota(shape, dim):
    return lax.broadcasted_iota(jnp.int32, shape, dim)


def column(row, size):
    diagonal = iota((size, size), 0) == iota((size, size), 1)
    return jnp.sum(jnp.where(diagonal, row, 0.0), axis=1, keepdims=True)


def dot(a, b):
    return jnp.dot(a, b, preferred_element_type=F32)


def kernel(
    nodes,
    locals_,
    cap,
    slot_ref,
    ids_ref,
    touched_ref,
    omap_ref,
    grads_hbm,
    moment_hbm,
    second_hbm,
    master_hbm,
    gath,
    gradient_out,
    grads,
    moment,
    second,
    master,
    route,
    route_t,
    collect,
    collect_t,
    select,
    part,
    up_src,
    up_dst,
    dn_src,
    dn_dst,
    fwd_src,
    fwd_dst,
    rep_src,
    rep_dst,
    load_sem,
    adam_sem,
    up_ss,
    up_rs,
    dn_ss,
    dn_rs,
    fwd_ss,
    fwd_rs,
    rep_ss,
    rep_rs,
    ag_up_ss,
    ag_dn_ss,
    ag_rs,
):
    n = lax.axis_index("node")
    j = lax.axis_index("local")
    last = locals_ - 1
    half = locals_ // 2
    width = grads.shape[1]
    cw = width // CHUNKS
    bw = cw // BLOCKS
    slots = part.shape[2]
    group = TILE // cap
    stacked = BLOCKS * slots

    loads = []
    for k in range(CHUNKS):
        cols = pl.ds(k * cw, cw)
        loads.append(
            pltpu.make_async_copy(grads_hbm.at[:, cols], grads.at[:, cols], load_sem.at[k])
        )
        loads[-1].start()
    adam_loads = [
        pltpu.make_async_copy(src, dst, adam_sem.at[i])
        for i, (src, dst) in enumerate(
            ((moment_hbm, moment), (second_hbm, second), (master_hbm, master))
        )
    ]
    for copy in adam_loads:
        copy.start()

    barrier = pltpu.get_barrier_semaphore()

    def greet(p):
        pl.semaphore_signal(
            barrier, inc=1, device_id=(lax.rem(n + p + 1, nodes), j), device_id_type=MESH
        )

    def greet_line(peer):
        pl.semaphore_signal(barrier, inc=1, device_id=(n, peer), device_id_type=MESH)

    tree = locals_ == 4
    inner = jnp.clip(j, 1, 2)
    outer = 3 * (inner - 1)
    far_inner, far_outer = 3 - inner, 3 - outer
    partner = inner + outer - j
    is_inner = j == inner
    if tree:
        greet_line(partner)
        greet_line(far_inner)
        pl.when(is_inner)(lambda: greet_line(far_outer))
        line_peers = 2 + jnp.minimum(j, 1) * jnp.minimum(last - j, 1)
    else:
        pl.when(j > 0)(lambda: greet_line(j - 1))
        pl.when(j < last)(lambda: greet_line(j + 1))
        line_peers = jnp.minimum(j, 1) + jnp.minimum(last - j, 1)
    repeat(nodes - 1, greet)

    shape = select.shape
    select[...] = jnp.where(iota(shape, 0) == slot_ref[...], 1.0, 0.0).astype(BF16)

    pl.semaphore_wait(barrier, nodes - 1 + line_peers)

    def up_copy(k, s):
        return pltpu.make_async_remote_copy(
            up_src.at[k, s],
            up_dst.at[k, s],
            up_ss.at[k, s],
            up_rs.at[k, s],
            device_id=(n, jnp.minimum(j + 1, last)),
            device_id_type=MESH,
        )

    def dn_copy(k, s):
        return pltpu.make_async_remote_copy(
            dn_src.at[k, s],
            dn_dst.at[k, s],
            dn_ss.at[k, s],
            dn_rs.at[k, s],
            device_id=(n, jnp.maximum(j - 1, 0)),
            device_id_type=MESH,
        )

    def ag_copy(k, t, up):
        rows = gath.at[pl.ds(pl.multiple_of(t * slots, slots), slots), pl.ds(k * cw, cw)]
        return pltpu.make_async_remote_copy(
            rows,
            rows,
            (ag_up_ss if up else ag_dn_ss).at[k, t],
            ag_rs.at[k, t],
            device_id=(n, jnp.minimum(j + 1, last) if up else jnp.maximum(j - 1, 0)),
            device_id_type=MESH,
        )

    def send_nodes(k, src, dst, ss, rs):
        def send(p):
            peer = lax.rem(n + p + 1, nodes)
            pltpu.make_async_remote_copy(
                src.at[k, peer],
                dst.at[k, n],
                ss.at[k],
                rs.at[k],
                device_id=(peer, j),
                device_id_type=MESH,
            ).start()

        repeat(nodes - 1, send)
        dst[k, n] = src[k, n]

    def wait_nodes(k, buf, sem):
        whole = buf.at[k, pl.ds(0, nodes - 1)]
        pltpu.make_async_copy(whole, whole, sem.at[k]).wait()

    def sums(k):
        loads[k].wait()
        total = dot(select[...], grads[:, k * cw : (k + 1) * cw])
        part[k] = total.reshape(locals_, slots, cw)

    def begin(k):
        sums(k)

        @pl.when(j == 0)
        def _():
            def step(s):
                up_src[k, s] = part[k, last - s].astype(BF16)
                up_copy(k, s).start()

            repeat(last, step)

        @pl.when(j == last)
        def _():
            def step(s):
                dn_src[k, s] = part[k, s].astype(BF16)
                dn_copy(k, s).start()

            repeat(last, step)

    def up_relay(k):
        def step(s):
            @pl.when(last - s > j)
            def _():
                up_copy(k, s).wait_recv()
                up_src[k, s] = (up_dst[k, s].astype(F32) + part[k, last - s]).astype(BF16)
                up_copy(k, s).start()

        repeat(last, step)

    def dn_relay(k):
        def step(s):
            @pl.when(s < j)
            def _():
                dn_copy(k, s).wait_recv()
                dn_src[k, s] = (dn_dst[k, s].astype(F32) + part[k, s]).astype(BF16)
                dn_copy(k, s).start()

        repeat(last, step)

    def near(k):
        pl.when((j > 0) & (j < half))(lambda: up_relay(k))
        pl.when((j < last) & (j >= half))(lambda: dn_relay(k))

    def far(k):
        pl.when((j > 0) & (j < half))(lambda: dn_relay(k))
        pl.when((j < last) & (j >= half))(lambda: up_relay(k))

    def forward(k):
        @pl.when(j > 0)
        def _():
            up_copy(k, last - j).wait_recv()
            part[k, j] = part[k, j] + up_dst[k, last - j].astype(F32)

        @pl.when(j < last)
        def _():
            dn_copy(k, j).wait_recv()
            part[k, j] = part[k, j] + dn_dst[k, j].astype(F32)

        send_out(k, part[k, j])

    def send_out(k, total):
        own = total.astype(BF16)
        tall = jnp.concatenate([own[:, b * bw : (b + 1) * bw] for b in range(BLOCKS)], axis=0)
        fwd_src[k] = dot(route[...], tall).astype(BF16).reshape(nodes, TILE, bw)
        send_nodes(k, fwd_src, fwd_dst, fwd_ss, fwd_rs)

    def update(k):
        if k == 0:
            for copy in adam_loads:
                copy.wait()
        wait_nodes(k, fwd_dst, fwd_rs)
        gradient = dot(collect[...], fwd_dst[k].reshape(nodes * TILE, bw))
        fresh = []
        for b in range(BLOCKS):
            cols = slice(k * cw + b * bw, k * cw + (b + 1) * bw)
            new = adam_rows(
                gradient[b * TILE : (b + 1) * TILE],
                moment[:, cols],
                second[:, cols],
                master[:, cols],
                kept,
            )
            gradient_out[:, cols] = gradient[b * TILE : (b + 1) * TILE]
            fresh.append(new[2].astype(BF16))
        tall = jnp.concatenate(fresh, axis=0)
        rep_src[k] = dot(collect_t[...], tall).astype(BF16).reshape(nodes, TILE, bw)
        send_nodes(k, rep_src, rep_dst, rep_ss, rep_rs)

    def fill(k):
        wait_nodes(k, rep_dst, rep_rs)
        rows = dot(route_t[...], rep_dst[k].reshape(nodes * TILE, bw)).astype(BF16)
        own = pl.ds(pl.multiple_of(j * slots, slots), slots)
        for b in range(BLOCKS):
            cols = slice(k * cw + b * bw, k * cw + (b + 1) * bw)
            gath[own, cols] = rows[b * slots : (b + 1) * slots]

    def listed(k):
        fill(k)

        @pl.when(j < last)
        def _():
            ag_copy(k, j, True).start()

        @pl.when(j > 0)
        def _():
            ag_copy(k, j, False).start()

    def pass_on(k, d):
        low, high = j - 1 - d, j + 1 + d

        @pl.when(low >= 0)
        def _():
            ag_copy(k, low, True).wait_recv()

            @pl.when(j < last)
            def _():
                ag_copy(k, low, True).start()

        @pl.when(high <= last)
        def _():
            ag_copy(k, high, False).wait_recv()

            @pl.when(j > 0)
            def _():
                ag_copy(k, high, False).start()

    def first_hop(k):
        pass_on(k, 0)

    def middle_hops(k):
        repeat(last - 2, lambda d: pass_on(k, d + 1))

    def last_hop(k):
        pass_on(k, last - 1)

    def pair_copy(k):
        rows = pl.ds(0, 2)
        return pltpu.make_async_remote_copy(
            up_src.at[k, rows],
            up_dst.at[k, rows],
            up_ss.at[k, 0],
            up_rs.at[k, 0],
            device_id=(n, partner),
            device_id_type=MESH,
        )

    def partner_copy(k):
        return pltpu.make_async_remote_copy(
            up_src.at[k, 2],
            up_dst.at[k, 2],
            up_ss.at[k, 2],
            up_rs.at[k, 1],
            device_id=(n, partner),
            device_id_type=MESH,
        )

    def far_copy(k, i):
        return pltpu.make_async_remote_copy(
            up_src.at[k, i],
            dn_dst.at[k, 0],
            up_ss.at[k, i],
            up_rs.at[k, 2],
            device_id=(n, far_outer if i else far_inner),
            device_id_type=MESH,
        )

    def row_copy(k, t, peer, i):
        rows = gath.at[pl.ds(pl.multiple_of(t * slots, slots), slots), pl.ds(k * cw, cw)]
        return pltpu.make_async_remote_copy(
            rows,
            rows,
            ag_up_ss.at[k, i],
            ag_rs.at[k, t],
            device_id=(n, peer),
            device_id_type=MESH,
        )

    def tree_begin(k):
        sums(k)

        @pl.when(~is_inner)
        def _():
            up_src[k, 0] = part[k, far_inner].astype(BF16)
            up_src[k, 1] = part[k, far_outer].astype(BF16)
            pair_copy(k).start()

        up_src[k, 2] = part[k, partner].astype(BF16)
        partner_copy(k).start()

    def merge(k):
        @pl.when(is_inner)
        def _():
            pair_copy(k).wait_recv()
            for i, t in enumerate((far_inner, far_outer)):
                up_src[k, i] = (up_dst[k, i].astype(F32) + part[k, t]).astype(BF16)
                far_copy(k, i).start()

    def tree_forward(k):
        partner_copy(k).wait_recv()
        far_copy(k, 0).wait_recv()
        send_out(k, part[k, j] + up_dst[k, 2].astype(F32) + dn_dst[k, 0].astype(F32))

    def tree_listed(k):
        fill(k)
        row_copy(k, j, far_inner, 0).start()
        row_copy(k, j, partner, 1).start()

    def tree_pass(k):
        @pl.when(is_inner)
        def _():
            for i, t in enumerate((far_inner, far_outer)):
                row_copy(k, t, partner, 2 + i).wait_recv()
                row_copy(k, t, partner, 2 + i).start()

    def tree_last(k):
        row_copy(k, partner, partner, 1).wait_recv()

        @pl.when(~is_inner)
        def _():
            for t in (far_inner, far_outer):
                row_copy(k, t, partner, 0).wait_recv()

    def tree_drain(k):
        @pl.when(is_inner)
        def _():
            for i in range(2):
                far_copy(k, i).wait_send()
                row_copy(k, far_outer if i else far_inner, partner, 2 + i).wait_send()

        @pl.when(~is_inner)
        def _():
            pair_copy(k).wait_send()

        partner_copy(k).wait_send()
        row_copy(k, j, far_inner, 0).wait_send()
        row_copy(k, j, partner, 1).wait_send()

    for k in range(CHUNKS):
        tree_begin(k) if tree else begin(k)

    rows_node = VOCAB // nodes
    owner = lax.shift_right_logical(ids_ref[...], rows_node.bit_length() - 1).astype(F32)
    shape = (slots, slots)
    earlier = (column(owner, slots) == owner) & (iota(shape, 0) < iota(shape, 1))
    rank = jnp.sum(jnp.where(earlier, 1.0, 0.0), axis=0, keepdims=True)
    sent = column(owner * float(cap) + rank, slots)
    shape = (slots, stacked)
    sent = jnp.sum(
        jnp.where(iota(shape, 0) == mod(iota(shape, 1), slots), sent, 0.0), axis=0, keepdims=True
    )
    shape = route.shape
    sub, lane = iota(shape, 0), iota(shape, 1)
    wanted = (div(sub, TILE) * cap + div(mod(sub, TILE), group)).astype(F32)
    routed = jnp.where((wanted == sent) & (mod(sub, group) == div(lane, slots)), 1.0, 0.0).astype(F32)
    route[...] = routed.astype(BF16)

    shape = (nodes, nodes * TILE)
    sub, lane = iota(shape, 0), iota(shape, 1)
    place = jnp.zeros((1, nodes * TILE), F32)
    for c in range(cap):
        held = column(omap_ref[c : c + 1, :].astype(F32), nodes)
        here = (sub == div(lane, TILE)) & (div(mod(lane, TILE), group) == c)
        place = place + jnp.sum(jnp.where(here, held, 0.0), axis=0, keepdims=True)
    shape = collect.shape
    sub, lane = iota(shape, 0), iota(shape, 1)
    taken = jnp.where(
        (mod(sub, TILE).astype(F32) == place) & (div(sub, TILE) == mod(lane, group)), 1.0, 0.0
    ).astype(F32)
    collect[...] = taken.astype(BF16)

    route_t[...] = routed.T.astype(BF16)
    collect_t[...] = taken.T.astype(BF16)
    kept = column(touched_ref[...].astype(F32), touched_ref.shape[1]) >= 0.0

    if tree:
        stages = (merge, tree_forward, update, tree_listed, tree_pass, tree_last)
    else:
        stages = (near, far, forward, update, listed, first_hop, middle_hops, last_hop)
    for tick in range(CHUNKS + len(stages) - 1):
        for depth in range(len(stages)):
            if 0 <= tick - depth < CHUNKS:
                stages[depth](tick - depth)

    for k in range(CHUNKS):
        wait_nodes(k, fwd_src, fwd_ss)
        wait_nodes(k, rep_src, rep_ss)
        if tree:
            tree_drain(k)
            continue

        def drain(s):
            @pl.when(last - s > j)
            def _():
                up_copy(k, s).wait_send()

            @pl.when(s < j)
            def _():
                dn_copy(k, s).wait_send()

        repeat(last, drain)

        def drain_gather(t):
            @pl.when((t <= j) & (j < last))
            def _():
                ag_copy(k, t, True).wait_send()

            @pl.when((t >= j) & (j > 0))
            def _():
                ag_copy(k, t, False).wait_send()

        repeat(locals_, drain_gather)


def write_kernel(
    slot_ref,
    touched_ref,
    rows,
    gradient,
    moment,
    second,
    master,
    tok_out,
    moment_out,
    second_out,
    master_out,
    select_t,
):
    @pl.when(pl.program_id(0) == 0)
    def _():
        shape = (rows.shape[0], tok_out.shape[0])
        chosen = jnp.where(iota(shape, 0) == slot_ref[...], 1.0, 0.0).astype(F32)
        select_t[...] = chosen.T.astype(BF16)

    kept = column(touched_ref[...].astype(F32), touched_ref.shape[1]) >= 0.0
    moment_out[...], second_out[...], master_out[...] = adam_rows(
        gradient[...], moment[...], second[...], master[...], kept
    )
    tok_out[...] = dot(select_t[...], rows[...]).astype(BF16)


def write_out(token_slot, touched_ids, rows, gradient, moment, second, master):
    tokens, touch = token_slot.shape[0], touched_ids.shape[0]
    list_len, width = rows.shape
    steps = 3
    block = width // steps

    def small(count):
        return pl.BlockSpec((1, count), lambda i: (0, 0))

    def tall(count):
        return pl.BlockSpec((count, block), lambda i: (0, i))

    return pl.pallas_call(
        write_kernel,
        grid=(steps,),
        out_shape=(jax.ShapeDtypeStruct((tokens, width), BF16),)
        + (jax.ShapeDtypeStruct((touch, width), F32),) * 3,
        in_specs=[small(tokens), small(touch), tall(list_len)] + [tall(touch)] * 4,
        out_specs=[tall(tokens)] + [tall(touch)] * 3,
        scratch_shapes=[pltpu.VMEM((tokens, list_len), BF16)],
        compiler_params=pltpu.CompilerParams(vmem_limit_bytes=56 * 1024 * 1024),
    )(
        token_slot.reshape(1, tokens),
        touched_ids.reshape(1, touch),
        rows,
        gradient,
        moment,
        second,
        master,
    )


def on_device(nodes, locals_, grads, token_slot, node_ids, touched_ids, owner_map, moment, second, master):
    tokens, width = grads.shape
    slots = node_ids.shape[1]
    touch = touched_ids.shape[0]
    cap = owner_map.shape[2]
    group = TILE // cap
    cw = width // CHUNKS
    bw = cw // BLOCKS
    last = locals_ - 1
    vmem = pl.BlockSpec(memory_space=pltpu.VMEM)
    hbm = pl.BlockSpec(memory_space=pltpu.HBM)
    dma = pltpu.SemaphoreType.DMA
    list_len = locals_ * slots
    line = pltpu.VMEM((CHUNKS, last, slots, cw), BF16)
    plane = pltpu.VMEM((CHUNKS, nodes, TILE, bw), BF16)
    stacked = BLOCKS * slots
    rows, gradient = pl.pallas_call(
        functools.partial(kernel, nodes, locals_, cap),
        out_shape=(
            jax.ShapeDtypeStruct((list_len, width), BF16),
            jax.ShapeDtypeStruct((touch, width), F32),
        ),
        in_specs=[vmem] * 4 + [hbm] * 4,
        out_specs=[vmem] * 2,
        scratch_shapes=[
            pltpu.VMEM((tokens, width), BF16),
            pltpu.VMEM((touch, width), F32),
            pltpu.VMEM((touch, width), F32),
            pltpu.VMEM((touch, width), F32),
            pltpu.VMEM((nodes * TILE, stacked), BF16),
            pltpu.VMEM((stacked, nodes * TILE), BF16),
            pltpu.VMEM((BLOCKS * touch, nodes * TILE), BF16),
            pltpu.VMEM((nodes * TILE, BLOCKS * touch), BF16),
            pltpu.VMEM((list_len, tokens), BF16),
            pltpu.VMEM((CHUNKS, locals_, slots, cw), F32),
            line,
            line,
            line,
            line,
            plane,
            plane,
            plane,
            plane,
            dma((CHUNKS,)),
            dma((3,)),
            dma((CHUNKS, last)),
            dma((CHUNKS, last)),
            dma((CHUNKS, last)),
            dma((CHUNKS, last)),
            dma((CHUNKS,)),
            dma((CHUNKS,)),
            dma((CHUNKS,)),
            dma((CHUNKS,)),
            dma((CHUNKS, locals_)),
            dma((CHUNKS, locals_)),
            dma((CHUNKS, locals_)),
        ],
        compiler_params=pltpu.CompilerParams(
            collective_id=0, has_side_effects=True, vmem_limit_bytes=56 * 1024 * 1024
        ),
    )(
        token_slot.reshape(1, tokens),
        node_ids,
        touched_ids.reshape(1, touch),
        jnp.swapaxes(owner_map, 1, 2).reshape(cap, nodes),
        grads,
        moment,
        second,
        master,
    )
    return write_out(token_slot, touched_ids, rows, gradient, moment, second, master)


def solution(mesh):
    nodes, locals_ = mesh.shape["node"], mesh.shape["local"]
    placed = (
        P(("node", "local"), None),
        P(("node", "local")),
        P("node", "local"),
        P(("node", "local")),
        P(("node", "local"), None, None),
        P(("node", "local"), None),
        P(("node", "local"), None),
        P(("node", "local"), None),
    )
    return jax.shard_map(
        functools.partial(on_device, nodes, locals_),
        mesh=mesh,
        in_specs=placed,
        out_specs=(P(("node", "local"), None),) * 4,
        check_vma=False,
    )
```

```python
import functools

import jax
import jax.numpy as jnp
from jax import lax
from jax.experimental import pallas as pl
from jax.experimental.pallas import tpu as pltpu
from jax.sharding import PartitionSpec as P

VOCAB = 262144
STEP = 100

BETA_ONE = 0.9
BETA_TWO = 0.999
LEARN_RATE = 0.01
EPSILON = 1e-08

MESH = pl.DeviceIdType.MESH
CHUNKS = 2
BLOCKS = 7
PIECES = 3
TILE = 16
F32 = jnp.float32
BF16 = jnp.bfloat16


def adam_rows(gradient, moment, second, master, kept):
    corr_one = 1.0 - BETA_ONE**STEP
    corr_two = 1.0 - BETA_TWO**STEP
    moment_new = BETA_ONE * moment + (1.0 - BETA_ONE) * gradient
    second_new = BETA_TWO * second + (1.0 - BETA_TWO) * gradient * gradient
    master_new = master - LEARN_RATE * (moment_new / corr_one) / (
        jnp.sqrt(second_new / corr_two) + EPSILON
    )
    return (
        jnp.where(kept, moment_new, moment),
        jnp.where(kept, second_new, second),
        jnp.where(kept, master_new, master),
    )


def repeat(count, body):
    if count <= 8:
        for step in range(count):
            body(step)
    else:
        lax.fori_loop(0, count, lambda step, carry: (body(step), carry)[1], None)


def div(x, m):
    return lax.shift_right_logical(x, m.bit_length() - 1) if m & (m - 1) == 0 else x // m


def mod(x, m):
    return x & (m - 1) if m & (m - 1) == 0 else x % m


def iota(shape, dim):
    return lax.broadcasted_iota(jnp.int32, shape, dim)


def column(row, size):
    diagonal = iota((size, size), 0) == iota((size, size), 1)
    return jnp.sum(jnp.where(diagonal, row, 0.0), axis=1, keepdims=True)


def dot(a, b):
    return jnp.dot(a, b, preferred_element_type=F32)


def kernel(
    nodes,
    locals_,
    cap,
    slot_ref,
    ids_ref,
    touched_ref,
    omap_ref,
    grads_hbm,
    moment_hbm,
    second_hbm,
    master_hbm,
    gath,
    gradient_out,
    grads,
    moment,
    second,
    master,
    route,
    route_t,
    collect,
    collect_t,
    select,
    part,
    up_src,
    up_dst,
    dn_src,
    dn_dst,
    fwd_src,
    fwd_dst,
    rep_src,
    rep_dst,
    load_sem,
    adam_sem,
    up_ss,
    up_rs,
    dn_ss,
    dn_rs,
    fwd_ss,
    fwd_rs,
    rep_ss,
    rep_rs,
    ag_up_ss,
    ag_dn_ss,
    ag_rs,
):
    n = lax.axis_index("node")
    j = lax.axis_index("local")
    last = locals_ - 1
    half = locals_ // 2
    width = grads.shape[1]
    cw = width // CHUNKS
    bw = cw // BLOCKS
    slots = part.shape[2]
    group = TILE // cap
    stacked = BLOCKS * slots

    loads = []
    for k in range(CHUNKS):
        cols = pl.ds(k * cw, cw)
        loads.append(
            pltpu.make_async_copy(grads_hbm.at[:, cols], grads.at[:, cols], load_sem.at[k])
        )
        loads[-1].start()
    adam_loads = [
        pltpu.make_async_copy(src, dst, adam_sem.at[i])
        for i, (src, dst) in enumerate(
            ((moment_hbm, moment), (second_hbm, second), (master_hbm, master))
        )
    ]
    for copy in adam_loads:
        copy.start()

    barrier = pltpu.get_barrier_semaphore()

    def greet(p):
        pl.semaphore_signal(
            barrier, inc=1, device_id=(lax.rem(n + p + 1, nodes), j), device_id_type=MESH
        )

    def greet_line(peer):
        pl.semaphore_signal(barrier, inc=1, device_id=(n, peer), device_id_type=MESH)

    tree = locals_ == 4
    inner = jnp.clip(j, 1, 2)
    outer = 3 * (inner - 1)
    far_inner, far_outer = 3 - inner, 3 - outer
    partner = inner + outer - j
    is_inner = j == inner
    if tree:
        greet_line(partner)
        greet_line(far_inner)
        pl.when(is_inner)(lambda: greet_line(far_outer))
        line_peers = 2 + jnp.minimum(j, 1) * jnp.minimum(last - j, 1)
    else:
        pl.when(j > 0)(lambda: greet_line(j - 1))
        pl.when(j < last)(lambda: greet_line(j + 1))
        line_peers = jnp.minimum(j, 1) + jnp.minimum(last - j, 1)
    repeat(nodes - 1, greet)

    shape = select.shape
    select[...] = jnp.where(iota(shape, 0) == slot_ref[...], 1.0, 0.0).astype(BF16)

    pl.semaphore_wait(barrier, nodes - 1 + line_peers)

    def up_copy(k, s):
        return pltpu.make_async_remote_copy(
            up_src.at[k, s],
            up_dst.at[k, s],
            up_ss.at[k, s],
            up_rs.at[k, s],
            device_id=(n, jnp.minimum(j + 1, last)),
            device_id_type=MESH,
        )

    def dn_copy(k, s):
        return pltpu.make_async_remote_copy(
            dn_src.at[k, s],
            dn_dst.at[k, s],
            dn_ss.at[k, s],
            dn_rs.at[k, s],
            device_id=(n, jnp.maximum(j - 1, 0)),
            device_id_type=MESH,
        )

    def ag_copy(k, t, up):
        rows = gath.at[pl.ds(pl.multiple_of(t * slots, slots), slots), pl.ds(k * cw, cw)]
        return pltpu.make_async_remote_copy(
            rows,
            rows,
            (ag_up_ss if up else ag_dn_ss).at[k, t],
            ag_rs.at[k, t],
            device_id=(n, jnp.minimum(j + 1, last) if up else jnp.maximum(j - 1, 0)),
            device_id_type=MESH,
        )

    def send_nodes(k, src, dst, ss, rs):
        def send(p):
            peer = lax.rem(n + p + 1, nodes)
            pltpu.make_async_remote_copy(
                src.at[k, peer],
                dst.at[k, n],
                ss.at[k],
                rs.at[k],
                device_id=(peer, j),
                device_id_type=MESH,
            ).start()

        repeat(nodes - 1, send)
        dst[k, n] = src[k, n]

    def wait_nodes(k, buf, sem):
        whole = buf.at[k, pl.ds(0, nodes - 1)]
        pltpu.make_async_copy(whole, whole, sem.at[k]).wait()

    def sums(k):
        loads[k].wait()
        total = dot(select[...], grads[:, k * cw : (k + 1) * cw])
        part[k] = total.reshape(locals_, slots, cw)

    def begin(k):
        sums(k)

        @pl.when(j == 0)
        def _():
            def step(s):
                up_src[k, s] = part[k, last - s].astype(BF16)
                up_copy(k, s).start()

            repeat(last, step)

        @pl.when(j == last)
        def _():
            def step(s):
                dn_src[k, s] = part[k, s].astype(BF16)
                dn_copy(k, s).start()

            repeat(last, step)

    def up_relay(k):
        def step(s):
            @pl.when(last - s > j)
            def _():
                up_copy(k, s).wait_recv()
                up_src[k, s] = (up_dst[k, s].astype(F32) + part[k, last - s]).astype(BF16)
                up_copy(k, s).start()

        repeat(last, step)

    def dn_relay(k):
        def step(s):
            @pl.when(s < j)
            def _():
                dn_copy(k, s).wait_recv()
                dn_src[k, s] = (dn_dst[k, s].astype(F32) + part[k, s]).astype(BF16)
                dn_copy(k, s).start()

        repeat(last, step)

    def near(k):
        pl.when((j > 0) & (j < half))(lambda: up_relay(k))
        pl.when((j < last) & (j >= half))(lambda: dn_relay(k))

    def far(k):
        pl.when((j > 0) & (j < half))(lambda: dn_relay(k))
        pl.when((j < last) & (j >= half))(lambda: up_relay(k))

    def forward(k):
        @pl.when(j > 0)
        def _():
            up_copy(k, last - j).wait_recv()
            part[k, j] = part[k, j] + up_dst[k, last - j].astype(F32)

        @pl.when(j < last)
        def _():
            dn_copy(k, j).wait_recv()
            part[k, j] = part[k, j] + dn_dst[k, j].astype(F32)

        send_out(k, part[k, j])

    def send_out(k, total):
        own = total.astype(BF16)
        tall = jnp.concatenate([own[:, b * bw : (b + 1) * bw] for b in range(BLOCKS)], axis=0)
        fwd_src[k] = dot(route[...], tall).astype(BF16).reshape(nodes, TILE, bw)
        send_nodes(k, fwd_src, fwd_dst, fwd_ss, fwd_rs)

    def update(k):
        if k == 0:
            for copy in adam_loads:
                copy.wait()
        wait_nodes(k, fwd_dst, fwd_rs)
        gradient = dot(collect[...], fwd_dst[k].reshape(nodes * TILE, bw))
        fresh = []
        for b in range(BLOCKS):
            cols = slice(k * cw + b * bw, k * cw + (b + 1) * bw)
            new = adam_rows(
                gradient[b * TILE : (b + 1) * TILE],
                moment[:, cols],
                second[:, cols],
                master[:, cols],
                kept,
            )
            gradient_out[:, cols] = gradient[b * TILE : (b + 1) * TILE]
            fresh.append(new[2].astype(BF16))
        tall = jnp.concatenate(fresh, axis=0)
        rep_src[k] = dot(collect_t[...], tall).astype(BF16).reshape(nodes, TILE, bw)
        send_nodes(k, rep_src, rep_dst, rep_ss, rep_rs)

    def fill(k):
        wait_nodes(k, rep_dst, rep_rs)
        rows = dot(route_t[...], rep_dst[k].reshape(nodes * TILE, bw)).astype(BF16)
        own = pl.ds(pl.multiple_of(j * slots, slots), slots)
        for b in range(BLOCKS):
            cols = slice(k * cw + b * bw, k * cw + (b + 1) * bw)
            gath[own, cols] = rows[b * slots : (b + 1) * slots]

    def listed(k):
        fill(k)

        @pl.when(j < last)
        def _():
            ag_copy(k, j, True).start()

        @pl.when(j > 0)
        def _():
            ag_copy(k, j, False).start()

    def pass_on(k, d):
        low, high = j - 1 - d, j + 1 + d

        @pl.when(low >= 0)
        def _():
            ag_copy(k, low, True).wait_recv()

            @pl.when(j < last)
            def _():
                ag_copy(k, low, True).start()

        @pl.when(high <= last)
        def _():
            ag_copy(k, high, False).wait_recv()

            @pl.when(j > 0)
            def _():
                ag_copy(k, high, False).start()

    def first_hop(k):
        pass_on(k, 0)

    def middle_hops(k):
        repeat(last - 2, lambda d: pass_on(k, d + 1))

    def last_hop(k):
        pass_on(k, last - 1)

    def pair_copy(k):
        rows = pl.ds(0, 2)
        return pltpu.make_async_remote_copy(
            up_src.at[k, rows],
            up_dst.at[k, rows],
            up_ss.at[k, 0],
            up_rs.at[k, 0],
            device_id=(n, partner),
            device_id_type=MESH,
        )

    def partner_copy(k):
        return pltpu.make_async_remote_copy(
            up_src.at[k, 2],
            up_dst.at[k, 2],
            up_ss.at[k, 2],
            up_rs.at[k, 1],
            device_id=(n, partner),
            device_id_type=MESH,
        )

    def far_copy(k, i):
        return pltpu.make_async_remote_copy(
            up_src.at[k, i],
            dn_dst.at[k, 0],
            up_ss.at[k, i],
            up_rs.at[k, 2],
            device_id=(n, far_outer if i else far_inner),
            device_id_type=MESH,
        )

    def row_copy(k, t, peer, i):
        rows = gath.at[pl.ds(pl.multiple_of(t * slots, slots), slots), pl.ds(k * cw, cw)]
        return pltpu.make_async_remote_copy(
            rows,
            rows,
            ag_up_ss.at[k, i],
            ag_rs.at[k, t],
            device_id=(n, peer),
            device_id_type=MESH,
        )

    def tree_begin(k):
        sums(k)

        @pl.when(~is_inner)
        def _():
            up_src[k, 0] = part[k, far_inner].astype(BF16)
            up_src[k, 1] = part[k, far_outer].astype(BF16)
            pair_copy(k).start()

        up_src[k, 2] = part[k, partner].astype(BF16)
        partner_copy(k).start()

    def merge(k):
        @pl.when(is_inner)
        def _():
            pair_copy(k).wait_recv()
            for i, t in enumerate((far_inner, far_outer)):
                up_src[k, i] = (up_dst[k, i].astype(F32) + part[k, t]).astype(BF16)
                far_copy(k, i).start()

    def tree_forward(k):
        partner_copy(k).wait_recv()
        far_copy(k, 0).wait_recv()
        send_out(k, part[k, j] + up_dst[k, 2].astype(F32) + dn_dst[k, 0].astype(F32))

    def tree_listed(k):
        fill(k)
        row_copy(k, j, far_inner, 0).start()
        row_copy(k, j, partner, 1).start()

    def tree_pass(k):
        @pl.when(is_inner)
        def _():
            for i, t in enumerate((far_inner, far_outer)):
                row_copy(k, t, partner, 2 + i).wait_recv()
                row_copy(k, t, partner, 2 + i).start()

    def tree_last(k):
        row_copy(k, partner, partner, 1).wait_recv()

        @pl.when(~is_inner)
        def _():
            for t in (far_inner, far_outer):
                row_copy(k, t, partner, 0).wait_recv()

    def tree_drain(k):
        @pl.when(is_inner)
        def _():
            for i in range(2):
                far_copy(k, i).wait_send()
                row_copy(k, far_outer if i else far_inner, partner, 2 + i).wait_send()

        @pl.when(~is_inner)
        def _():
            pair_copy(k).wait_send()

        partner_copy(k).wait_send()
        row_copy(k, j, far_inner, 0).wait_send()
        row_copy(k, j, partner, 1).wait_send()

    for k in range(CHUNKS):
        tree_begin(k) if tree else begin(k)

    rows_node = VOCAB // nodes
    owner = lax.shift_right_logical(ids_ref[...], rows_node.bit_length() - 1).astype(F32)
    shape = (slots, slots)
    earlier = (column(owner, slots) == owner) & (iota(shape, 0) < iota(shape, 1))
    rank = jnp.sum(jnp.where(earlier, 1.0, 0.0), axis=0, keepdims=True)
    sent = column(owner * float(cap) + rank, slots)
    shape = (slots, stacked)
    sent = jnp.sum(
        jnp.where(iota(shape, 0) == mod(iota(shape, 1), slots), sent, 0.0), axis=0, keepdims=True
    )
    shape = route.shape
    sub, lane = iota(shape, 0), iota(shape, 1)
    wanted = (div(sub, TILE) * cap + div(mod(sub, TILE), group)).astype(F32)
    routed = jnp.where((wanted == sent) & (mod(sub, group) == div(lane, slots)), 1.0, 0.0).astype(F32)
    route[...] = routed.astype(BF16)

    shape = (nodes, nodes * TILE)
    sub, lane = iota(shape, 0), iota(shape, 1)
    place = jnp.zeros((1, nodes * TILE), F32)
    for c in range(cap):
        held = column(omap_ref[c : c + 1, :].astype(F32), nodes)
        here = (sub == div(lane, TILE)) & (div(mod(lane, TILE), group) == c)
        place = place + jnp.sum(jnp.where(here, held, 0.0), axis=0, keepdims=True)
    shape = collect.shape
    sub, lane = iota(shape, 0), iota(shape, 1)
    taken = jnp.where(
        (mod(sub, TILE).astype(F32) == place) & (div(sub, TILE) == mod(lane, group)), 1.0, 0.0
    ).astype(F32)
    collect[...] = taken.astype(BF16)

    route_t[...] = routed.T.astype(BF16)
    collect_t[...] = taken.T.astype(BF16)
    kept = column(touched_ref[...].astype(F32), touched_ref.shape[1]) >= 0.0

    if tree:
        stages = (merge, tree_forward, update, tree_listed, tree_pass, tree_last)
    else:
        stages = (near, far, forward, update, listed, first_hop, middle_hops, last_hop)
    for tick in range(CHUNKS + len(stages) - 1):
        for depth in range(len(stages)):
            if 0 <= tick - depth < CHUNKS:
                stages[depth](tick - depth)

    for k in range(CHUNKS):
        wait_nodes(k, fwd_src, fwd_ss)
        wait_nodes(k, rep_src, rep_ss)
        if tree:
            tree_drain(k)
            continue

        def drain(s):
            @pl.when(last - s > j)
            def _():
                up_copy(k, s).wait_send()

            @pl.when(s < j)
            def _():
                dn_copy(k, s).wait_send()

        repeat(last, drain)

        def drain_gather(t):
            @pl.when((t <= j) & (j < last))
            def _():
                ag_copy(k, t, True).wait_send()

            @pl.when((t >= j) & (j > 0))
            def _():
                ag_copy(k, t, False).wait_send()

        repeat(locals_, drain_gather)


def write_kernel(
    slot_ref,
    touched_ref,
    rows_hbm,
    gradient_hbm,
    moment_hbm,
    second_hbm,
    master_hbm,
    tok_hbm,
    moment_out_hbm,
    second_out_hbm,
    master_out_hbm,
    rows,
    states,
    tok,
    news,
    rows_sem,
    state_sem,
    tok_sem,
    new_sem,
):
    width = rows.shape[1]
    block = width // PIECES
    pieces = [pl.ds(p * block, block) for p in range(PIECES)]
    row_loads = [
        pltpu.make_async_copy(rows_hbm.at[:, c], rows.at[:, c], rows_sem.at[p])
        for p, c in enumerate(pieces)
    ]
    state_loads = [
        pltpu.make_async_copy(ref, states.at[i], state_sem.at[i])
        for i, ref in enumerate((gradient_hbm, moment_hbm, second_hbm, master_hbm))
    ]
    for copy in row_loads + state_loads:
        copy.start()
    shape = (rows.shape[0], tok.shape[0])
    chosen = jnp.where(iota(shape, 0) == slot_ref[...], 1.0, 0.0).astype(F32)
    select_t = chosen.T.astype(BF16)
    kept = column(touched_ref[...].astype(F32), touched_ref.shape[1]) >= 0.0
    stores = []
    for p, c in enumerate(pieces):
        row_loads[p].wait()
        tok[:, c] = dot(select_t, rows[:, c]).astype(BF16)
        stores.append(pltpu.make_async_copy(tok.at[:, c], tok_hbm.at[:, c], tok_sem.at[p]))
        stores[-1].start()
    for copy in state_loads:
        copy.wait()
    for p, c in enumerate(pieces):
        new = adam_rows(states[0, :, c], states[1, :, c], states[2, :, c], states[3, :, c], kept)
        outs = (moment_out_hbm, second_out_hbm, master_out_hbm)
        for i, (value, out) in enumerate(zip(new, outs)):
            news[i, :, c] = value
            stores.append(
                pltpu.make_async_copy(news.at[i, :, c], out.at[:, c], new_sem.at[i, p])
            )
            stores[-1].start()
    for copy in stores:
        copy.wait()


def write_out(token_slot, touched_ids, rows, gradient, moment, second, master):
    tokens, touch = token_slot.shape[0], touched_ids.shape[0]
    list_len, width = rows.shape
    vmem = pl.BlockSpec(memory_space=pltpu.VMEM)
    hbm = pl.BlockSpec(memory_space=pltpu.HBM)
    dma = pltpu.SemaphoreType.DMA
    return pl.pallas_call(
        write_kernel,
        out_shape=(jax.ShapeDtypeStruct((tokens, width), BF16),)
        + (jax.ShapeDtypeStruct((touch, width), F32),) * 3,
        in_specs=[vmem] * 2 + [hbm] * 5,
        out_specs=[hbm] * 4,
        scratch_shapes=[
            pltpu.VMEM((list_len, width), BF16),
            pltpu.VMEM((4, touch, width), F32),
            pltpu.VMEM((tokens, width), BF16),
            pltpu.VMEM((3, touch, width), F32),
            dma((PIECES,)),
            dma((4,)),
            dma((PIECES,)),
            dma((3, PIECES)),
        ],
        compiler_params=pltpu.CompilerParams(vmem_limit_bytes=56 * 1024 * 1024),
    )(
        token_slot.reshape(1, tokens),
        touched_ids.reshape(1, touch),
        rows,
        gradient,
        moment,
        second,
        master,
    )


def on_device(nodes, locals_, grads, token_slot, node_ids, touched_ids, owner_map, moment, second, master):
    tokens, width = grads.shape
    slots = node_ids.shape[1]
    touch = touched_ids.shape[0]
    cap = owner_map.shape[2]
    group = TILE // cap
    cw = width // CHUNKS
    bw = cw // BLOCKS
    last = locals_ - 1
    vmem = pl.BlockSpec(memory_space=pltpu.VMEM)
    hbm = pl.BlockSpec(memory_space=pltpu.HBM)
    dma = pltpu.SemaphoreType.DMA
    list_len = locals_ * slots
    line = pltpu.VMEM((CHUNKS, last, slots, cw), BF16)
    plane = pltpu.VMEM((CHUNKS, nodes, TILE, bw), BF16)
    stacked = BLOCKS * slots
    rows, gradient = pl.pallas_call(
        functools.partial(kernel, nodes, locals_, cap),
        out_shape=(
            jax.ShapeDtypeStruct((list_len, width), BF16),
            jax.ShapeDtypeStruct((touch, width), F32),
        ),
        in_specs=[vmem] * 4 + [hbm] * 4,
        out_specs=[vmem] * 2,
        scratch_shapes=[
            pltpu.VMEM((tokens, width), BF16),
            pltpu.VMEM((touch, width), F32),
            pltpu.VMEM((touch, width), F32),
            pltpu.VMEM((touch, width), F32),
            pltpu.VMEM((nodes * TILE, stacked), BF16),
            pltpu.VMEM((stacked, nodes * TILE), BF16),
            pltpu.VMEM((BLOCKS * touch, nodes * TILE), BF16),
            pltpu.VMEM((nodes * TILE, BLOCKS * touch), BF16),
            pltpu.VMEM((list_len, tokens), BF16),
            pltpu.VMEM((CHUNKS, locals_, slots, cw), F32),
            line,
            line,
            line,
            line,
            plane,
            plane,
            plane,
            plane,
            dma((CHUNKS,)),
            dma((3,)),
            dma((CHUNKS, last)),
            dma((CHUNKS, last)),
            dma((CHUNKS, last)),
            dma((CHUNKS, last)),
            dma((CHUNKS,)),
            dma((CHUNKS,)),
            dma((CHUNKS,)),
            dma((CHUNKS,)),
            dma((CHUNKS, locals_)),
            dma((CHUNKS, locals_)),
            dma((CHUNKS, locals_)),
        ],
        compiler_params=pltpu.CompilerParams(
            collective_id=0, has_side_effects=True, vmem_limit_bytes=56 * 1024 * 1024
        ),
    )(
        token_slot.reshape(1, tokens),
        node_ids,
        touched_ids.reshape(1, touch),
        jnp.swapaxes(owner_map, 1, 2).reshape(cap, nodes),
        grads,
        moment,
        second,
        master,
    )
    return write_out(token_slot, touched_ids, rows, gradient, moment, second, master)


def solution(mesh):
    nodes, locals_ = mesh.shape["node"], mesh.shape["local"]
    placed = (
        P(("node", "local"), None),
        P(("node", "local")),
        P("node", "local"),
        P(("node", "local")),
        P(("node", "local"), None, None),
        P(("node", "local"), None),
        P(("node", "local"), None),
        P(("node", "local"), None),
    )
    return jax.shard_map(
        functools.partial(on_device, nodes, locals_),
        mesh=mesh,
        in_specs=placed,
        out_specs=(P(("node", "local"), None),) * 4,
        check_vma=False,
    )
```

```python
import functools

import jax
import jax.numpy as jnp
from jax import lax
from jax.experimental import pallas as pl
from jax.experimental.pallas import tpu as pltpu
from jax.sharding import PartitionSpec as P

VOCAB = 262144
STEP = 100

BETA_ONE = 0.9
BETA_TWO = 0.999
LEARN_RATE = 0.01
EPSILON = 1e-08

MESH = pl.DeviceIdType.MESH
SHARES = (1, 2, 2, 1)
CHUNKS = len(SHARES)
BLOCKS = 7
PIECES = 3
TILE = 16
F32 = jnp.float32
BF16 = jnp.bfloat16


def adam_rows(gradient, moment, second, master, kept):
    corr_one = 1.0 - BETA_ONE**STEP
    corr_two = 1.0 - BETA_TWO**STEP
    moment_new = BETA_ONE * moment + (1.0 - BETA_ONE) * gradient
    second_new = BETA_TWO * second + (1.0 - BETA_TWO) * gradient * gradient
    master_new = master - LEARN_RATE * (moment_new / corr_one) / (
        jnp.sqrt(second_new / corr_two) + EPSILON
    )
    return (
        jnp.where(kept, moment_new, moment),
        jnp.where(kept, second_new, second),
        jnp.where(kept, master_new, master),
    )


def repeat(count, body):
    if count <= 8:
        for step in range(count):
            body(step)
    else:
        lax.fori_loop(0, count, lambda step, carry: (body(step), carry)[1], None)


def div(x, m):
    return lax.shift_right_logical(x, m.bit_length() - 1) if m & (m - 1) == 0 else x // m


def mod(x, m):
    return x & (m - 1) if m & (m - 1) == 0 else x % m


def iota(shape, dim):
    return lax.broadcasted_iota(jnp.int32, shape, dim)


def column(row, size):
    diagonal = iota((size, size), 0) == iota((size, size), 1)
    return jnp.sum(jnp.where(diagonal, row, 0.0), axis=1, keepdims=True)


def dot(a, b):
    return jnp.dot(a, b, preferred_element_type=F32)


def chunk_widths(width):
    unit = width // sum(SHARES)
    cws = [unit * share for share in SHARES]
    return cws, [sum(cws[:k]) for k in range(CHUNKS)]


def kernel(
    nodes,
    locals_,
    cap,
    slot_ref,
    ids_ref,
    touched_ref,
    omap_ref,
    grads_hbm,
    moment_hbm,
    second_hbm,
    master_hbm,
    gath,
    gradient_out,
    grads,
    moment,
    second,
    master,
    route,
    route_t,
    collect,
    collect_t,
    select,
    part,
    up_src,
    up_dst,
    dn_src,
    dn_dst,
    fwd_src,
    fwd_dst,
    rep_src,
    rep_dst,
    load_sem,
    adam_sem,
    up_ss,
    up_rs,
    dn_ss,
    dn_rs,
    fwd_ss,
    fwd_rs,
    rep_ss,
    rep_rs,
    ag_up_ss,
    ag_dn_ss,
    ag_rs,
):
    n = lax.axis_index("node")
    j = lax.axis_index("local")
    last = locals_ - 1
    half = locals_ // 2
    width = grads.shape[1]
    cws, starts = chunk_widths(width)
    bws = [cw // BLOCKS for cw in cws]
    slots = part[0].shape[1]
    group = TILE // cap
    stacked = BLOCKS * slots

    loads = []
    for k in range(CHUNKS):
        cols = pl.ds(starts[k], cws[k])
        loads.append(
            pltpu.make_async_copy(grads_hbm.at[:, cols], grads.at[:, cols], load_sem.at[k])
        )
        loads[-1].start()
    adam_loads = [
        pltpu.make_async_copy(src, dst, adam_sem.at[i])
        for i, (src, dst) in enumerate(
            ((moment_hbm, moment), (second_hbm, second), (master_hbm, master))
        )
    ]
    for copy in adam_loads:
        copy.start()

    barrier = pltpu.get_barrier_semaphore()

    def greet(p):
        pl.semaphore_signal(
            barrier, inc=1, device_id=(lax.rem(n + p + 1, nodes), j), device_id_type=MESH
        )

    def greet_line(peer):
        pl.semaphore_signal(barrier, inc=1, device_id=(n, peer), device_id_type=MESH)

    tree = locals_ == 4
    inner = jnp.clip(j, 1, 2)
    outer = 3 * (inner - 1)
    far_inner, far_outer = 3 - inner, 3 - outer
    partner = inner + outer - j
    is_inner = j == inner
    if tree:
        greet_line(partner)
        greet_line(far_inner)
        pl.when(is_inner)(lambda: greet_line(far_outer))
        line_peers = 2 + jnp.minimum(j, 1) * jnp.minimum(last - j, 1)
    else:
        pl.when(j > 0)(lambda: greet_line(j - 1))
        pl.when(j < last)(lambda: greet_line(j + 1))
        line_peers = jnp.minimum(j, 1) + jnp.minimum(last - j, 1)
    repeat(nodes - 1, greet)

    shape = select.shape
    select[...] = jnp.where(iota(shape, 0) == slot_ref[...], 1.0, 0.0).astype(BF16)

    pl.semaphore_wait(barrier, nodes - 1 + line_peers)

    def up_copy(k, s):
        return pltpu.make_async_remote_copy(
            up_src[k].at[s],
            up_dst[k].at[s],
            up_ss.at[k, s],
            up_rs.at[k, s],
            device_id=(n, jnp.minimum(j + 1, last)),
            device_id_type=MESH,
        )

    def dn_copy(k, s):
        return pltpu.make_async_remote_copy(
            dn_src[k].at[s],
            dn_dst[k].at[s],
            dn_ss.at[k, s],
            dn_rs.at[k, s],
            device_id=(n, jnp.maximum(j - 1, 0)),
            device_id_type=MESH,
        )

    def ag_copy(k, t, up):
        rows = gath.at[pl.ds(pl.multiple_of(t * slots, slots), slots), pl.ds(starts[k], cws[k])]
        return pltpu.make_async_remote_copy(
            rows,
            rows,
            (ag_up_ss if up else ag_dn_ss).at[k, t],
            ag_rs.at[k, t],
            device_id=(n, jnp.minimum(j + 1, last) if up else jnp.maximum(j - 1, 0)),
            device_id_type=MESH,
        )

    def send_nodes(k, src, dst, ss, rs):
        def send(p):
            peer = lax.rem(n + p + 1, nodes)
            pltpu.make_async_remote_copy(
                src[k].at[peer],
                dst[k].at[n],
                ss.at[k],
                rs.at[k],
                device_id=(peer, j),
                device_id_type=MESH,
            ).start()

        repeat(nodes - 1, send)
        dst[k][n] = src[k][n]

    def wait_nodes(k, buf, sem):
        whole = buf[k].at[pl.ds(0, nodes - 1)]
        pltpu.make_async_copy(whole, whole, sem.at[k]).wait()

    def sums(k):
        loads[k].wait()
        total = dot(select[...], grads[:, starts[k] : starts[k] + cws[k]])
        part[k][...] = total.reshape(locals_, slots, cws[k])

    def begin(k):
        sums(k)

        @pl.when(j == 0)
        def _():
            def step(s):
                up_src[k][s] = part[k][last - s].astype(BF16)
                up_copy(k, s).start()

            repeat(last, step)

        @pl.when(j == last)
        def _():
            def step(s):
                dn_src[k][s] = part[k][s].astype(BF16)
                dn_copy(k, s).start()

            repeat(last, step)

    def up_relay(k):
        def step(s):
            @pl.when(last - s > j)
            def _():
                up_copy(k, s).wait_recv()
                up_src[k][s] = (up_dst[k][s].astype(F32) + part[k][last - s]).astype(BF16)
                up_copy(k, s).start()

        repeat(last, step)

    def dn_relay(k):
        def step(s):
            @pl.when(s < j)
            def _():
                dn_copy(k, s).wait_recv()
                dn_src[k][s] = (dn_dst[k][s].astype(F32) + part[k][s]).astype(BF16)
                dn_copy(k, s).start()

        repeat(last, step)

    def near(k):
        pl.when((j > 0) & (j < half))(lambda: up_relay(k))
        pl.when((j < last) & (j >= half))(lambda: dn_relay(k))

    def far(k):
        pl.when((j > 0) & (j < half))(lambda: dn_relay(k))
        pl.when((j < last) & (j >= half))(lambda: up_relay(k))

    def forward(k):
        @pl.when(j > 0)
        def _():
            up_copy(k, last - j).wait_recv()
            part[k][j] = part[k][j] + up_dst[k][last - j].astype(F32)

        @pl.when(j < last)
        def _():
            dn_copy(k, j).wait_recv()
            part[k][j] = part[k][j] + dn_dst[k][j].astype(F32)

        send_out(k, part[k][j])

    def send_out(k, total):
        own = total.astype(BF16)
        tall = jnp.concatenate([own[:, b * bws[k] : (b + 1) * bws[k]] for b in range(BLOCKS)], axis=0)
        fwd_src[k][...] = dot(route[...], tall).astype(BF16).reshape(nodes, TILE, bws[k])
        send_nodes(k, fwd_src, fwd_dst, fwd_ss, fwd_rs)

    def update(k):
        if k == 0:
            for copy in adam_loads:
                copy.wait()
        wait_nodes(k, fwd_dst, fwd_rs)
        gradient = dot(collect[...], fwd_dst[k][...].reshape(nodes * TILE, bws[k]))
        fresh = []
        for b in range(BLOCKS):
            cols = slice(starts[k] + b * bws[k], starts[k] + (b + 1) * bws[k])
            new = adam_rows(
                gradient[b * TILE : (b + 1) * TILE],
                moment[:, cols],
                second[:, cols],
                master[:, cols],
                kept,
            )
            gradient_out[:, cols] = gradient[b * TILE : (b + 1) * TILE]
            fresh.append(new[2].astype(BF16))
        tall = jnp.concatenate(fresh, axis=0)
        rep_src[k][...] = dot(collect_t[...], tall).astype(BF16).reshape(nodes, TILE, bws[k])
        send_nodes(k, rep_src, rep_dst, rep_ss, rep_rs)

    def fill(k):
        wait_nodes(k, rep_dst, rep_rs)
        rows = dot(route_t[...], rep_dst[k][...].reshape(nodes * TILE, bws[k])).astype(BF16)
        own = pl.ds(pl.multiple_of(j * slots, slots), slots)
        for b in range(BLOCKS):
            cols = slice(starts[k] + b * bws[k], starts[k] + (b + 1) * bws[k])
            gath[own, cols] = rows[b * slots : (b + 1) * slots]

    def listed(k):
        fill(k)

        @pl.when(j < last)
        def _():
            ag_copy(k, j, True).start()

        @pl.when(j > 0)
        def _():
            ag_copy(k, j, False).start()

    def pass_on(k, d):
        low, high = j - 1 - d, j + 1 + d

        @pl.when(low >= 0)
        def _():
            ag_copy(k, low, True).wait_recv()

            @pl.when(j < last)
            def _():
                ag_copy(k, low, True).start()

        @pl.when(high <= last)
        def _():
            ag_copy(k, high, False).wait_recv()

            @pl.when(j > 0)
            def _():
                ag_copy(k, high, False).start()

    def first_hop(k):
        pass_on(k, 0)

    def middle_hops(k):
        repeat(last - 2, lambda d: pass_on(k, d + 1))

    def last_hop(k):
        pass_on(k, last - 1)

    def pair_copy(k):
        rows = pl.ds(0, 2)
        return pltpu.make_async_remote_copy(
            up_src[k].at[rows],
            up_dst[k].at[rows],
            up_ss.at[k, 0],
            up_rs.at[k, 0],
            device_id=(n, partner),
            device_id_type=MESH,
        )

    def partner_copy(k):
        return pltpu.make_async_remote_copy(
            up_src[k].at[2],
            up_dst[k].at[2],
            up_ss.at[k, 2],
            up_rs.at[k, 1],
            device_id=(n, partner),
            device_id_type=MESH,
        )

    def far_copy(k, i):
        return pltpu.make_async_remote_copy(
            up_src[k].at[i],
            dn_dst[k].at[0],
            up_ss.at[k, i],
            up_rs.at[k, 2],
            device_id=(n, far_outer if i else far_inner),
            device_id_type=MESH,
        )

    def row_copy(k, t, peer, i):
        rows = gath.at[pl.ds(pl.multiple_of(t * slots, slots), slots), pl.ds(starts[k], cws[k])]
        return pltpu.make_async_remote_copy(
            rows,
            rows,
            ag_up_ss.at[k, i],
            ag_rs.at[k, t],
            device_id=(n, peer),
            device_id_type=MESH,
        )

    def tree_begin(k):
        sums(k)

        @pl.when(~is_inner)
        def _():
            up_src[k][0] = part[k][far_inner].astype(BF16)
            up_src[k][1] = part[k][far_outer].astype(BF16)
            pair_copy(k).start()

        up_src[k][2] = part[k][partner].astype(BF16)
        partner_copy(k).start()

    def merge(k):
        @pl.when(is_inner)
        def _():
            pair_copy(k).wait_recv()
            for i, t in enumerate((far_inner, far_outer)):
                up_src[k][i] = (up_dst[k][i].astype(F32) + part[k][t]).astype(BF16)
                far_copy(k, i).start()

    def tree_forward(k):
        partner_copy(k).wait_recv()
        far_copy(k, 0).wait_recv()
        send_out(k, part[k][j] + up_dst[k][2].astype(F32) + dn_dst[k][0].astype(F32))

    def tree_listed(k):
        fill(k)
        row_copy(k, j, far_inner, 0).start()
        row_copy(k, j, partner, 1).start()

    def tree_pass(k):
        @pl.when(is_inner)
        def _():
            for i, t in enumerate((far_inner, far_outer)):
                row_copy(k, t, partner, 2 + i).wait_recv()
                row_copy(k, t, partner, 2 + i).start()

    def tree_last(k):
        row_copy(k, partner, partner, 1).wait_recv()

        @pl.when(~is_inner)
        def _():
            for t in (far_inner, far_outer):
                row_copy(k, t, partner, 0).wait_recv()

    def tree_drain(k):
        @pl.when(is_inner)
        def _():
            for i in range(2):
                far_copy(k, i).wait_send()
                row_copy(k, far_outer if i else far_inner, partner, 2 + i).wait_send()

        @pl.when(~is_inner)
        def _():
            pair_copy(k).wait_send()

        partner_copy(k).wait_send()
        row_copy(k, j, far_inner, 0).wait_send()
        row_copy(k, j, partner, 1).wait_send()

    for k in range(CHUNKS):
        tree_begin(k) if tree else begin(k)

    rows_node = VOCAB // nodes
    owner = lax.shift_right_logical(ids_ref[...], rows_node.bit_length() - 1).astype(F32)
    shape = (slots, slots)
    earlier = (column(owner, slots) == owner) & (iota(shape, 0) < iota(shape, 1))
    rank = jnp.sum(jnp.where(earlier, 1.0, 0.0), axis=0, keepdims=True)
    sent = column(owner * float(cap) + rank, slots)
    shape = (slots, stacked)
    sent = jnp.sum(
        jnp.where(iota(shape, 0) == mod(iota(shape, 1), slots), sent, 0.0), axis=0, keepdims=True
    )
    shape = route.shape
    sub, lane = iota(shape, 0), iota(shape, 1)
    wanted = (div(sub, TILE) * cap + div(mod(sub, TILE), group)).astype(F32)
    routed = jnp.where((wanted == sent) & (mod(sub, group) == div(lane, slots)), 1.0, 0.0).astype(F32)
    route[...] = routed.astype(BF16)

    shape = (nodes, nodes * TILE)
    sub, lane = iota(shape, 0), iota(shape, 1)
    place = jnp.zeros((1, nodes * TILE), F32)
    for c in range(cap):
        held = column(omap_ref[c : c + 1, :].astype(F32), nodes)
        here = (sub == div(lane, TILE)) & (div(mod(lane, TILE), group) == c)
        place = place + jnp.sum(jnp.where(here, held, 0.0), axis=0, keepdims=True)
    shape = collect.shape
    sub, lane = iota(shape, 0), iota(shape, 1)
    taken = jnp.where(
        (mod(sub, TILE).astype(F32) == place) & (div(sub, TILE) == mod(lane, group)), 1.0, 0.0
    ).astype(F32)
    collect[...] = taken.astype(BF16)

    route_t[...] = routed.T.astype(BF16)
    collect_t[...] = taken.T.astype(BF16)
    kept = column(touched_ref[...].astype(F32), touched_ref.shape[1]) >= 0.0

    if tree:
        stages = (merge, tree_forward, update, tree_listed, tree_pass, tree_last)
    else:
        stages = (near, far, forward, update, listed, first_hop, middle_hops, last_hop)
    for tick in range(CHUNKS + len(stages) - 1):
        for depth in range(len(stages)):
            if 0 <= tick - depth < CHUNKS:
                stages[depth](tick - depth)

    for k in range(CHUNKS):
        wait_nodes(k, fwd_src, fwd_ss)
        wait_nodes(k, rep_src, rep_ss)
        if tree:
            tree_drain(k)
            continue

        def drain(s):
            @pl.when(last - s > j)
            def _():
                up_copy(k, s).wait_send()

            @pl.when(s < j)
            def _():
                dn_copy(k, s).wait_send()

        repeat(last, drain)

        def drain_gather(t):
            @pl.when((t <= j) & (j < last))
            def _():
                ag_copy(k, t, True).wait_send()

            @pl.when((t >= j) & (j > 0))
            def _():
                ag_copy(k, t, False).wait_send()

        repeat(locals_, drain_gather)


def write_kernel(
    slot_ref,
    touched_ref,
    rows_hbm,
    gradient_hbm,
    moment_hbm,
    second_hbm,
    master_hbm,
    tok_hbm,
    moment_out_hbm,
    second_out_hbm,
    master_out_hbm,
    rows,
    states,
    tok,
    news,
    rows_sem,
    state_sem,
    tok_sem,
    new_sem,
):
    width = rows.shape[1]
    block = width // PIECES
    pieces = [pl.ds(p * block, block) for p in range(PIECES)]
    row_loads = [
        pltpu.make_async_copy(rows_hbm.at[:, c], rows.at[:, c], rows_sem.at[p])
        for p, c in enumerate(pieces)
    ]
    state_loads = [
        pltpu.make_async_copy(ref, states.at[i], state_sem.at[i])
        for i, ref in enumerate((gradient_hbm, moment_hbm, second_hbm, master_hbm))
    ]
    for copy in row_loads + state_loads:
        copy.start()
    shape = (rows.shape[0], tok.shape[0])
    chosen = jnp.where(iota(shape, 0) == slot_ref[...], 1.0, 0.0).astype(F32)
    select_t = chosen.T.astype(BF16)
    kept = column(touched_ref[...].astype(F32), touched_ref.shape[1]) >= 0.0
    stores = []
    for p, c in enumerate(pieces):
        row_loads[p].wait()
        tok[:, c] = dot(select_t, rows[:, c]).astype(BF16)
        stores.append(pltpu.make_async_copy(tok.at[:, c], tok_hbm.at[:, c], tok_sem.at[p]))
        stores[-1].start()
    for copy in state_loads:
        copy.wait()
    for p, c in enumerate(pieces):
        new = adam_rows(states[0, :, c], states[1, :, c], states[2, :, c], states[3, :, c], kept)
        outs = (moment_out_hbm, second_out_hbm, master_out_hbm)
        for i, (value, out) in enumerate(zip(new, outs)):
            news[i, :, c] = value
            stores.append(
                pltpu.make_async_copy(news.at[i, :, c], out.at[:, c], new_sem.at[i, p])
            )
            stores[-1].start()
    for copy in stores:
        copy.wait()


def write_out(token_slot, touched_ids, rows, gradient, moment, second, master):
    tokens, touch = token_slot.shape[0], touched_ids.shape[0]
    list_len, width = rows.shape
    vmem = pl.BlockSpec(memory_space=pltpu.VMEM)
    hbm = pl.BlockSpec(memory_space=pltpu.HBM)
    dma = pltpu.SemaphoreType.DMA
    return pl.pallas_call(
        write_kernel,
        out_shape=(jax.ShapeDtypeStruct((tokens, width), BF16),)
        + (jax.ShapeDtypeStruct((touch, width), F32),) * 3,
        in_specs=[vmem] * 2 + [hbm] * 5,
        out_specs=[hbm] * 4,
        scratch_shapes=[
            pltpu.VMEM((list_len, width), BF16),
            pltpu.VMEM((4, touch, width), F32),
            pltpu.VMEM((tokens, width), BF16),
            pltpu.VMEM((3, touch, width), F32),
            dma((PIECES,)),
            dma((4,)),
            dma((PIECES,)),
            dma((3, PIECES)),
        ],
        compiler_params=pltpu.CompilerParams(vmem_limit_bytes=56 * 1024 * 1024),
    )(
        token_slot.reshape(1, tokens),
        touched_ids.reshape(1, touch),
        rows,
        gradient,
        moment,
        second,
        master,
    )


def on_device(nodes, locals_, grads, token_slot, node_ids, touched_ids, owner_map, moment, second, master):
    tokens, width = grads.shape
    slots = node_ids.shape[1]
    touch = touched_ids.shape[0]
    cap = owner_map.shape[2]
    group = TILE // cap
    cws, _ = chunk_widths(width)
    last = locals_ - 1
    vmem = pl.BlockSpec(memory_space=pltpu.VMEM)
    hbm = pl.BlockSpec(memory_space=pltpu.HBM)
    dma = pltpu.SemaphoreType.DMA
    list_len = locals_ * slots
    line = tuple(pltpu.VMEM((last, slots, cw), BF16) for cw in cws)
    plane = tuple(pltpu.VMEM((nodes, TILE, cw // BLOCKS), BF16) for cw in cws)
    stacked = BLOCKS * slots
    rows, gradient = pl.pallas_call(
        functools.partial(kernel, nodes, locals_, cap),
        out_shape=(
            jax.ShapeDtypeStruct((list_len, width), BF16),
            jax.ShapeDtypeStruct((touch, width), F32),
        ),
        in_specs=[vmem] * 4 + [hbm] * 4,
        out_specs=[vmem] * 2,
        scratch_shapes=[
            pltpu.VMEM((tokens, width), BF16),
            pltpu.VMEM((touch, width), F32),
            pltpu.VMEM((touch, width), F32),
            pltpu.VMEM((touch, width), F32),
            pltpu.VMEM((nodes * TILE, stacked), BF16),
            pltpu.VMEM((stacked, nodes * TILE), BF16),
            pltpu.VMEM((BLOCKS * touch, nodes * TILE), BF16),
            pltpu.VMEM((nodes * TILE, BLOCKS * touch), BF16),
            pltpu.VMEM((list_len, tokens), BF16),
            tuple(pltpu.VMEM((locals_, slots, cw), F32) for cw in cws),
            line,
            line,
            line,
            line,
            plane,
            plane,
            plane,
            plane,
            dma((CHUNKS,)),
            dma((3,)),
            dma((CHUNKS, last)),
            dma((CHUNKS, last)),
            dma((CHUNKS, last)),
            dma((CHUNKS, last)),
            dma((CHUNKS,)),
            dma((CHUNKS,)),
            dma((CHUNKS,)),
            dma((CHUNKS,)),
            dma((CHUNKS, locals_)),
            dma((CHUNKS, locals_)),
            dma((CHUNKS, locals_)),
        ],
        compiler_params=pltpu.CompilerParams(
            collective_id=0, has_side_effects=True, vmem_limit_bytes=56 * 1024 * 1024
        ),
    )(
        token_slot.reshape(1, tokens),
        node_ids,
        touched_ids.reshape(1, touch),
        jnp.swapaxes(owner_map, 1, 2).reshape(cap, nodes),
        grads,
        moment,
        second,
        master,
    )
    return write_out(token_slot, touched_ids, rows, gradient, moment, second, master)


def solution(mesh):
    nodes, locals_ = mesh.shape["node"], mesh.shape["local"]
    placed = (
        P(("node", "local"), None),
        P(("node", "local")),
        P("node", "local"),
        P(("node", "local")),
        P(("node", "local"), None, None),
        P(("node", "local"), None),
        P(("node", "local"), None),
        P(("node", "local"), None),
    )
    return jax.shard_map(
        functools.partial(on_device, nodes, locals_),
        mesh=mesh,
        in_specs=placed,
        out_specs=(P(("node", "local"), None),) * 4,
        check_vma=False,
    )
```

```python
import functools

import jax
import jax.numpy as jnp
from jax import lax
from jax.experimental import pallas as pl
from jax.experimental.pallas import tpu as pltpu
from jax.sharding import PartitionSpec as P

VOCAB = 262144
STEP = 100

BETA_ONE = 0.9
BETA_TWO = 0.999
LEARN_RATE = 0.01
EPSILON = 1e-08

MESH = pl.DeviceIdType.MESH
SHARES = (2, 2, 2)
CHUNKS = len(SHARES)
BLOCKS = 7
PIECES = 3
TILE = 16
F32 = jnp.float32
BF16 = jnp.bfloat16


def adam_rows(gradient, moment, second, master, kept):
    corr_one = 1.0 - BETA_ONE**STEP
    corr_two = 1.0 - BETA_TWO**STEP
    moment_new = BETA_ONE * moment + (1.0 - BETA_ONE) * gradient
    second_new = BETA_TWO * second + (1.0 - BETA_TWO) * gradient * gradient
    master_new = master - LEARN_RATE * (moment_new / corr_one) / (
        jnp.sqrt(second_new / corr_two) + EPSILON
    )
    return (
        jnp.where(kept, moment_new, moment),
        jnp.where(kept, second_new, second),
        jnp.where(kept, master_new, master),
    )


def repeat(count, body):
    if count <= 8:
        for step in range(count):
            body(step)
    else:
        lax.fori_loop(0, count, lambda step, carry: (body(step), carry)[1], None)


def div(x, m):
    return lax.shift_right_logical(x, m.bit_length() - 1) if m & (m - 1) == 0 else x // m


def mod(x, m):
    return x & (m - 1) if m & (m - 1) == 0 else x % m


def iota(shape, dim):
    return lax.broadcasted_iota(jnp.int32, shape, dim)


def column(row, size):
    diagonal = iota((size, size), 0) == iota((size, size), 1)
    return jnp.sum(jnp.where(diagonal, row, 0.0), axis=1, keepdims=True)


def dot(a, b):
    return jnp.dot(a, b, preferred_element_type=F32)


def chunk_widths(width):
    unit = width // sum(SHARES)
    cws = [unit * share for share in SHARES]
    return cws, [sum(cws[:k]) for k in range(CHUNKS)]


def kernel(
    nodes,
    locals_,
    cap,
    slot_ref,
    ids_ref,
    touched_ref,
    omap_ref,
    grads_hbm,
    moment_hbm,
    second_hbm,
    master_hbm,
    gath,
    moment_hbm_out,
    second_hbm_out,
    master_hbm_out,
    grads,
    moment,
    second,
    master,
    route,
    route_t,
    collect,
    collect_t,
    select,
    part,
    up_src,
    up_dst,
    dn_src,
    dn_dst,
    fwd_src,
    fwd_dst,
    rep_src,
    rep_dst,
    load_sem,
    adam_sem,
    state_sem,
    up_ss,
    up_rs,
    dn_ss,
    dn_rs,
    fwd_ss,
    fwd_rs,
    rep_ss,
    rep_rs,
    ag_up_ss,
    ag_dn_ss,
    ag_rs,
):
    n = lax.axis_index("node")
    j = lax.axis_index("local")
    last = locals_ - 1
    half = locals_ // 2
    width = grads.shape[1]
    cws, starts = chunk_widths(width)
    bws = [cw // BLOCKS for cw in cws]
    slots = part[0].shape[1]
    group = TILE // cap
    stacked = BLOCKS * slots

    loads = []
    for k in range(CHUNKS):
        cols = pl.ds(starts[k], cws[k])
        loads.append(
            pltpu.make_async_copy(grads_hbm.at[:, cols], grads.at[:, cols], load_sem.at[k])
        )
        loads[-1].start()
    adam_loads = [
        pltpu.make_async_copy(src, dst, adam_sem.at[i])
        for i, (src, dst) in enumerate(
            ((moment_hbm, moment), (second_hbm, second), (master_hbm, master))
        )
    ]
    for copy in adam_loads:
        copy.start()
    state_stores = [
        pltpu.make_async_copy(src, dst, state_sem.at[i])
        for i, (src, dst) in enumerate(
            ((moment, moment_hbm_out), (second, second_hbm_out), (master, master_hbm_out))
        )
    ]

    barrier = pltpu.get_barrier_semaphore()

    def greet(p):
        pl.semaphore_signal(
            barrier, inc=1, device_id=(lax.rem(n + p + 1, nodes), j), device_id_type=MESH
        )

    def greet_line(peer):
        pl.semaphore_signal(barrier, inc=1, device_id=(n, peer), device_id_type=MESH)

    tree = locals_ == 4
    inner = jnp.clip(j, 1, 2)
    outer = 3 * (inner - 1)
    far_inner, far_outer = 3 - inner, 3 - outer
    partner = inner + outer - j
    is_inner = j == inner
    if tree:
        greet_line(partner)
        greet_line(far_inner)
        pl.when(is_inner)(lambda: greet_line(far_outer))
        line_peers = 2 + jnp.minimum(j, 1) * jnp.minimum(last - j, 1)
    else:
        pl.when(j > 0)(lambda: greet_line(j - 1))
        pl.when(j < last)(lambda: greet_line(j + 1))
        line_peers = jnp.minimum(j, 1) + jnp.minimum(last - j, 1)
    repeat(nodes - 1, greet)

    shape = select.shape
    select[...] = jnp.where(iota(shape, 0) == slot_ref[...], 1.0, 0.0).astype(BF16)

    pl.semaphore_wait(barrier, nodes - 1 + line_peers)

    def up_copy(k, s):
        return pltpu.make_async_remote_copy(
            up_src[k].at[s],
            up_dst[k].at[s],
            up_ss.at[k, s],
            up_rs.at[k, s],
            device_id=(n, jnp.minimum(j + 1, last)),
            device_id_type=MESH,
        )

    def dn_copy(k, s):
        return pltpu.make_async_remote_copy(
            dn_src[k].at[s],
            dn_dst[k].at[s],
            dn_ss.at[k, s],
            dn_rs.at[k, s],
            device_id=(n, jnp.maximum(j - 1, 0)),
            device_id_type=MESH,
        )

    def ag_copy(k, t, up):
        rows = gath.at[pl.ds(pl.multiple_of(t * slots, slots), slots), pl.ds(starts[k], cws[k])]
        return pltpu.make_async_remote_copy(
            rows,
            rows,
            (ag_up_ss if up else ag_dn_ss).at[k, t],
            ag_rs.at[k, t],
            device_id=(n, jnp.minimum(j + 1, last) if up else jnp.maximum(j - 1, 0)),
            device_id_type=MESH,
        )

    def send_nodes(k, src, dst, ss, rs):
        def send(p):
            peer = lax.rem(n + p + 1, nodes)
            pltpu.make_async_remote_copy(
                src[k].at[peer],
                dst[k].at[n],
                ss.at[k],
                rs.at[k],
                device_id=(peer, j),
                device_id_type=MESH,
            ).start()

        repeat(nodes - 1, send)
        dst[k][n] = src[k][n]

    def wait_nodes(k, buf, sem):
        whole = buf[k].at[pl.ds(0, nodes - 1)]
        pltpu.make_async_copy(whole, whole, sem.at[k]).wait()

    def sums(k):
        loads[k].wait()
        total = dot(select[...], grads[:, starts[k] : starts[k] + cws[k]])
        part[k][...] = total.reshape(locals_, slots, cws[k])

    def begin(k):
        sums(k)

        @pl.when(j == 0)
        def _():
            def step(s):
                up_src[k][s] = part[k][last - s].astype(BF16)
                up_copy(k, s).start()

            repeat(last, step)

        @pl.when(j == last)
        def _():
            def step(s):
                dn_src[k][s] = part[k][s].astype(BF16)
                dn_copy(k, s).start()

            repeat(last, step)

    def up_relay(k):
        def step(s):
            @pl.when(last - s > j)
            def _():
                up_copy(k, s).wait_recv()
                up_src[k][s] = (up_dst[k][s].astype(F32) + part[k][last - s]).astype(BF16)
                up_copy(k, s).start()

        repeat(last, step)

    def dn_relay(k):
        def step(s):
            @pl.when(s < j)
            def _():
                dn_copy(k, s).wait_recv()
                dn_src[k][s] = (dn_dst[k][s].astype(F32) + part[k][s]).astype(BF16)
                dn_copy(k, s).start()

        repeat(last, step)

    def near(k):
        pl.when((j > 0) & (j < half))(lambda: up_relay(k))
        pl.when((j < last) & (j >= half))(lambda: dn_relay(k))

    def far(k):
        pl.when((j > 0) & (j < half))(lambda: dn_relay(k))
        pl.when((j < last) & (j >= half))(lambda: up_relay(k))

    def forward(k):
        @pl.when(j > 0)
        def _():
            up_copy(k, last - j).wait_recv()
            part[k][j] = part[k][j] + up_dst[k][last - j].astype(F32)

        @pl.when(j < last)
        def _():
            dn_copy(k, j).wait_recv()
            part[k][j] = part[k][j] + dn_dst[k][j].astype(F32)

        send_out(k, part[k][j])

    def send_out(k, total):
        own = total.astype(BF16)
        tall = jnp.concatenate([own[:, b * bws[k] : (b + 1) * bws[k]] for b in range(BLOCKS)], axis=0)
        fwd_src[k][...] = dot(route[...], tall).astype(BF16).reshape(nodes, TILE, bws[k])
        send_nodes(k, fwd_src, fwd_dst, fwd_ss, fwd_rs)

    def update(k):
        if k == 0:
            for copy in adam_loads:
                copy.wait()
        wait_nodes(k, fwd_dst, fwd_rs)
        gradient = dot(collect[...], fwd_dst[k][...].reshape(nodes * TILE, bws[k]))
        fresh = []
        for b in range(BLOCKS):
            cols = slice(starts[k] + b * bws[k], starts[k] + (b + 1) * bws[k])
            new = adam_rows(
                gradient[b * TILE : (b + 1) * TILE],
                moment[:, cols],
                second[:, cols],
                master[:, cols],
                kept,
            )
            moment[:, cols], second[:, cols], master[:, cols] = new
            fresh.append(new[2].astype(BF16))
        if k == CHUNKS - 1:
            for copy in state_stores:
                copy.start()
        tall = jnp.concatenate(fresh, axis=0)
        rep_src[k][...] = dot(collect_t[...], tall).astype(BF16).reshape(nodes, TILE, bws[k])
        send_nodes(k, rep_src, rep_dst, rep_ss, rep_rs)

    def fill(k):
        wait_nodes(k, rep_dst, rep_rs)
        rows = dot(route_t[...], rep_dst[k][...].reshape(nodes * TILE, bws[k])).astype(BF16)
        own = pl.ds(pl.multiple_of(j * slots, slots), slots)
        for b in range(BLOCKS):
            cols = slice(starts[k] + b * bws[k], starts[k] + (b + 1) * bws[k])
            gath[own, cols] = rows[b * slots : (b + 1) * slots]

    def listed(k):
        fill(k)

        @pl.when(j < last)
        def _():
            ag_copy(k, j, True).start()

        @pl.when(j > 0)
        def _():
            ag_copy(k, j, False).start()

    def pass_on(k, d):
        low, high = j - 1 - d, j + 1 + d

        @pl.when(low >= 0)
        def _():
            ag_copy(k, low, True).wait_recv()

            @pl.when(j < last)
            def _():
                ag_copy(k, low, True).start()

        @pl.when(high <= last)
        def _():
            ag_copy(k, high, False).wait_recv()

            @pl.when(j > 0)
            def _():
                ag_copy(k, high, False).start()

    def first_hop(k):
        pass_on(k, 0)

    def middle_hops(k):
        repeat(last - 2, lambda d: pass_on(k, d + 1))

    def last_hop(k):
        pass_on(k, last - 1)

    def pair_copy(k):
        rows = pl.ds(0, 2)
        return pltpu.make_async_remote_copy(
            up_src[k].at[rows],
            up_dst[k].at[rows],
            up_ss.at[k, 0],
            up_rs.at[k, 0],
            device_id=(n, partner),
            device_id_type=MESH,
        )

    def partner_copy(k):
        return pltpu.make_async_remote_copy(
            up_src[k].at[2],
            up_dst[k].at[2],
            up_ss.at[k, 2],
            up_rs.at[k, 1],
            device_id=(n, partner),
            device_id_type=MESH,
        )

    def far_copy(k, i):
        return pltpu.make_async_remote_copy(
            up_src[k].at[i],
            dn_dst[k].at[0],
            up_ss.at[k, i],
            up_rs.at[k, 2],
            device_id=(n, far_outer if i else far_inner),
            device_id_type=MESH,
        )

    def row_copy(k, t, peer, i):
        rows = gath.at[pl.ds(pl.multiple_of(t * slots, slots), slots), pl.ds(starts[k], cws[k])]
        return pltpu.make_async_remote_copy(
            rows,
            rows,
            ag_up_ss.at[k, i],
            ag_rs.at[k, t],
            device_id=(n, peer),
            device_id_type=MESH,
        )

    def tree_begin(k):
        sums(k)

        @pl.when(~is_inner)
        def _():
            up_src[k][0] = part[k][far_inner].astype(BF16)
            up_src[k][1] = part[k][far_outer].astype(BF16)
            pair_copy(k).start()

        up_src[k][2] = part[k][partner].astype(BF16)
        partner_copy(k).start()

    def merge(k):
        @pl.when(is_inner)
        def _():
            pair_copy(k).wait_recv()
            for i, t in enumerate((far_inner, far_outer)):
                up_src[k][i] = (up_dst[k][i].astype(F32) + part[k][t]).astype(BF16)
                far_copy(k, i).start()

    def tree_forward(k):
        partner_copy(k).wait_recv()
        far_copy(k, 0).wait_recv()
        send_out(k, part[k][j] + up_dst[k][2].astype(F32) + dn_dst[k][0].astype(F32))

    def tree_listed(k):
        fill(k)
        row_copy(k, j, far_inner, 0).start()
        row_copy(k, j, partner, 1).start()

    def tree_pass(k):
        @pl.when(is_inner)
        def _():
            for i, t in enumerate((far_inner, far_outer)):
                row_copy(k, t, partner, 2 + i).wait_recv()
                row_copy(k, t, partner, 2 + i).start()

    def tree_last(k):
        row_copy(k, partner, partner, 1).wait_recv()

        @pl.when(~is_inner)
        def _():
            for t in (far_inner, far_outer):
                row_copy(k, t, partner, 0).wait_recv()

    def tree_drain(k):
        @pl.when(is_inner)
        def _():
            for i in range(2):
                far_copy(k, i).wait_send()
                row_copy(k, far_outer if i else far_inner, partner, 2 + i).wait_send()

        @pl.when(~is_inner)
        def _():
            pair_copy(k).wait_send()

        partner_copy(k).wait_send()
        row_copy(k, j, far_inner, 0).wait_send()
        row_copy(k, j, partner, 1).wait_send()

    for k in range(CHUNKS):
        tree_begin(k) if tree else begin(k)

    rows_node = VOCAB // nodes
    owner = lax.shift_right_logical(ids_ref[...], rows_node.bit_length() - 1).astype(F32)
    shape = (slots, slots)
    earlier = (column(owner, slots) == owner) & (iota(shape, 0) < iota(shape, 1))
    rank = jnp.sum(jnp.where(earlier, 1.0, 0.0), axis=0, keepdims=True)
    sent = column(owner * float(cap) + rank, slots)
    shape = (slots, stacked)
    sent = jnp.sum(
        jnp.where(iota(shape, 0) == mod(iota(shape, 1), slots), sent, 0.0), axis=0, keepdims=True
    )
    shape = route.shape
    sub, lane = iota(shape, 0), iota(shape, 1)
    wanted = (div(sub, TILE) * cap + div(mod(sub, TILE), group)).astype(F32)
    routed = jnp.where((wanted == sent) & (mod(sub, group) == div(lane, slots)), 1.0, 0.0).astype(F32)
    route[...] = routed.astype(BF16)

    shape = (nodes, nodes * TILE)
    sub, lane = iota(shape, 0), iota(shape, 1)
    place = jnp.zeros((1, nodes * TILE), F32)
    for c in range(cap):
        held = column(omap_ref[c : c + 1, :].astype(F32), nodes)
        here = (sub == div(lane, TILE)) & (div(mod(lane, TILE), group) == c)
        place = place + jnp.sum(jnp.where(here, held, 0.0), axis=0, keepdims=True)
    shape = collect.shape
    sub, lane = iota(shape, 0), iota(shape, 1)
    taken = jnp.where(
        (mod(sub, TILE).astype(F32) == place) & (div(sub, TILE) == mod(lane, group)), 1.0, 0.0
    ).astype(F32)
    collect[...] = taken.astype(BF16)

    route_t[...] = routed.T.astype(BF16)
    collect_t[...] = taken.T.astype(BF16)
    kept = column(touched_ref[...].astype(F32), touched_ref.shape[1]) >= 0.0

    if tree:
        stages = (merge, tree_forward, update, tree_listed, tree_pass, tree_last)
    else:
        stages = (near, far, forward, update, listed, first_hop, middle_hops, last_hop)
    for tick in range(CHUNKS + len(stages) - 1):
        for depth in range(len(stages)):
            if 0 <= tick - depth < CHUNKS:
                stages[depth](tick - depth)

    for copy in state_stores:
        copy.wait()

    for k in range(CHUNKS):
        wait_nodes(k, fwd_src, fwd_ss)
        wait_nodes(k, rep_src, rep_ss)
        if tree:
            tree_drain(k)
            continue

        def drain(s):
            @pl.when(last - s > j)
            def _():
                up_copy(k, s).wait_send()

            @pl.when(s < j)
            def _():
                dn_copy(k, s).wait_send()

        repeat(last, drain)

        def drain_gather(t):
            @pl.when((t <= j) & (j < last))
            def _():
                ag_copy(k, t, True).wait_send()

            @pl.when((t >= j) & (j > 0))
            def _():
                ag_copy(k, t, False).wait_send()

        repeat(locals_, drain_gather)


def write_kernel(
    slot_ref,
    rows_hbm,
    moment_hbm,
    second_hbm,
    master_hbm,
    tok_hbm,
    moment_out,
    second_out,
    master_out,
    rows,
    tok,
    rows_sem,
    state_sem,
    tok_sem,
):
    width = rows.shape[1]
    block = width // PIECES
    pieces = [pl.ds(p * block, block) for p in range(PIECES)]
    row_loads = [
        pltpu.make_async_copy(rows_hbm.at[:, c], rows.at[:, c], rows_sem.at[p])
        for p, c in enumerate(pieces)
    ]
    stores = [
        pltpu.make_async_copy(src, dst, state_sem.at[i])
        for i, (src, dst) in enumerate(
            ((moment_hbm, moment_out), (second_hbm, second_out), (master_hbm, master_out))
        )
    ]
    for copy in row_loads + stores:
        copy.start()
    shape = (rows.shape[0], tok.shape[0])
    chosen = jnp.where(iota(shape, 0) == slot_ref[...], 1.0, 0.0).astype(F32)
    select_t = chosen.T.astype(BF16)
    for p, c in enumerate(pieces):
        row_loads[p].wait()
        tok[:, c] = dot(select_t, rows[:, c]).astype(BF16)
        stores.append(pltpu.make_async_copy(tok.at[:, c], tok_hbm.at[:, c], tok_sem.at[p]))
        stores[-1].start()
    for copy in stores:
        copy.wait()


def write_out(token_slot, rows, moment, second, master):
    tokens, touch = token_slot.shape[0], moment.shape[0]
    list_len, width = rows.shape
    vmem = pl.BlockSpec(memory_space=pltpu.VMEM)
    hbm = pl.BlockSpec(memory_space=pltpu.HBM)
    dma = pltpu.SemaphoreType.DMA
    return pl.pallas_call(
        write_kernel,
        out_shape=(jax.ShapeDtypeStruct((tokens, width), BF16),)
        + (jax.ShapeDtypeStruct((touch, width), F32),) * 3,
        in_specs=[vmem] + [hbm] * 4,
        out_specs=[hbm] * 4,
        scratch_shapes=[
            pltpu.VMEM((list_len, width), BF16),
            pltpu.VMEM((tokens, width), BF16),
            dma((PIECES,)),
            dma((3,)),
            dma((PIECES,)),
        ],
        compiler_params=pltpu.CompilerParams(vmem_limit_bytes=56 * 1024 * 1024),
    )(token_slot.reshape(1, tokens), rows, moment, second, master)


def on_device(nodes, locals_, grads, token_slot, node_ids, touched_ids, owner_map, moment, second, master):
    tokens, width = grads.shape
    slots = node_ids.shape[1]
    touch = touched_ids.shape[0]
    cap = owner_map.shape[2]
    group = TILE // cap
    cws, _ = chunk_widths(width)
    last = locals_ - 1
    vmem = pl.BlockSpec(memory_space=pltpu.VMEM)
    hbm = pl.BlockSpec(memory_space=pltpu.HBM)
    dma = pltpu.SemaphoreType.DMA
    list_len = locals_ * slots
    line = tuple(pltpu.VMEM((last, slots, cw), BF16) for cw in cws)
    plane = tuple(pltpu.VMEM((nodes, TILE, cw // BLOCKS), BF16) for cw in cws)
    stacked = BLOCKS * slots
    rows, *states = pl.pallas_call(
        functools.partial(kernel, nodes, locals_, cap),
        out_shape=(
            jax.ShapeDtypeStruct((list_len, width), BF16),
        )
        + (jax.ShapeDtypeStruct((touch, width), F32),) * 3,
        in_specs=[vmem] * 4 + [hbm] * 4,
        out_specs=[vmem] + [hbm] * 3,
        scratch_shapes=[
            pltpu.VMEM((tokens, width), BF16),
            pltpu.VMEM((touch, width), F32),
            pltpu.VMEM((touch, width), F32),
            pltpu.VMEM((touch, width), F32),
            pltpu.VMEM((nodes * TILE, stacked), BF16),
            pltpu.VMEM((stacked, nodes * TILE), BF16),
            pltpu.VMEM((BLOCKS * touch, nodes * TILE), BF16),
            pltpu.VMEM((nodes * TILE, BLOCKS * touch), BF16),
            pltpu.VMEM((list_len, tokens), BF16),
            tuple(pltpu.VMEM((locals_, slots, cw), F32) for cw in cws),
            line,
            line,
            line,
            line,
            plane,
            plane,
            plane,
            plane,
            dma((CHUNKS,)),
            dma((3,)),
            dma((3,)),
            dma((CHUNKS, last)),
            dma((CHUNKS, last)),
            dma((CHUNKS, last)),
            dma((CHUNKS, last)),
            dma((CHUNKS,)),
            dma((CHUNKS,)),
            dma((CHUNKS,)),
            dma((CHUNKS,)),
            dma((CHUNKS, locals_)),
            dma((CHUNKS, locals_)),
            dma((CHUNKS, locals_)),
        ],
        compiler_params=pltpu.CompilerParams(
            collective_id=0, has_side_effects=True, vmem_limit_bytes=56 * 1024 * 1024
        ),
    )(
        token_slot.reshape(1, tokens),
        node_ids,
        touched_ids.reshape(1, touch),
        jnp.swapaxes(owner_map, 1, 2).reshape(cap, nodes),
        grads,
        moment,
        second,
        master,
    )
    return write_out(token_slot, rows, *states)


def solution(mesh):
    nodes, locals_ = mesh.shape["node"], mesh.shape["local"]
    placed = (
        P(("node", "local"), None),
        P(("node", "local")),
        P("node", "local"),
        P(("node", "local")),
        P(("node", "local"), None, None),
        P(("node", "local"), None),
        P(("node", "local"), None),
        P(("node", "local"), None),
    )
    return jax.shard_map(
        functools.partial(on_device, nodes, locals_),
        mesh=mesh,
        in_specs=placed,
        out_specs=(P(("node", "local"), None),) * 4,
        check_vma=False,
    )
```
